1024 devices in a mesh: sub: 64 (over z, core), dom: 16 (over y, x).
Axes of the slice: x: 4, y: 4, z: 32, core: 2. Of those that a mesh axis runs over, the one named last changes fastest.
Arguments:
- loads: float32 [64, 16, 1024, 128], P('sub', 'dom'), may hold values from -6 to 6
- coefficient: float32 [64, 16], P('sub', 'dom'), may hold values from 0.5 to 4
- schur_ref: bfloat16 [1024, 1024], replicated, as said below
- schur_inverse: bfloat16 [64, 16, 1024, 1024], P('sub', 'dom'), as said below
- coarse_basis: bfloat16 [64, 16, 1024, 96], P('sub', 'dom'), may hold values from -0.1875 to 0.1875
- partners: int32 [64, 16, 2, 8], P('sub', 'dom'), may hold values from 0 to 15, as said below
- routes: int32 [64, 16, 96, 1], P('sub', 'dom'), may hold values from 0 to 63; in each aligned block of 96 rows (0 to 95, 96 to 191, ..., all dimensions but the last counted through in order) at most 2 rows name the same one
- coarse_rows: int32 [64, 16, 96], P('sub', 'dom'), may hold values from 0 to 63
- primal_count: int32 [64, 16], P('sub', 'dom'), may hold values from 48 to 96
- coarse_inverse: float32 [64, 16, 64, 64], P('sub', 'dom'), as said below
Outputs:
- solution: float32 [64, 16, 1024, 128], P('sub', 'dom')
The draws below stay inside these ranges and needn't reach their ends.
Inputs may be any that keep to these rules, and one draw needn't show every extreme that they name: `partners`: every subdomain has 8 tiles, each shared with exactly one other subdomain of its group as described in the reference program; the pair numbers of one subdomain are distinct; one subdomain shares at most 1 tiles with any one other, and that many with some. `routes`: among the 96 listed primal rows of one subdomain at most 2 name one coarse group, and some subdomain has exactly 2 for some group. `schur_ref`: symmetric and positive definite. `schur_inverse`: each block symmetric and positive definite. `coarse_inverse`: each block symmetric and positive definite.
All inputs are finite; a program needn't handle non-finite values.
Results may differ from the reference program's by a relative error of at most 0.0012.
Values sent between devices are 32-bit elements; how exact they have to be, the bound alone decides.
No kernel may reach another device: no remote copies, remote signals or barrier semaphores. Data moves between devices by JAX's collectives and lax.ppermute only.
A program may use at most 32 MiB of HBM per device.

```python
import math
import jax
import jax.numpy as jnp
import numpy as np
from jax import lax

NI = 1024
TILE = 128
K = 128
PMAX = 96
CROWS = 64
ITERS = 2
GROUPS = 64
MEMBERS = 16
NT = 8
PCAP = 2


def spd_blocks(key, shape, low, high, spread):
    first_key, second_key = jax.random.split(key)
    noise_raw = jax.random.normal(first_key, shape, jnp.float32)
    symmetric = (noise_raw + jnp.swapaxes(noise_raw, -1, -2)) * (spread / 1.4142 / shape[-1] ** 0.5)
    diagonal = jax.random.uniform(second_key, shape[:-1], jnp.float32, low, high)
    return symmetric + diagonal[..., None] * jnp.eye(shape[-1], dtype=jnp.float32)


def draw_schur_ref(key, part):
    key = jax.random.fold_in(key, 11)
    return spd_blocks(key, (NI, NI), 4.0, 8.0, 1.6).astype(jnp.bfloat16)


def draw_schur_inverse(key, part):
    key = jax.random.fold_in(key, 12)
    return spd_blocks(key, (GROUPS, MEMBERS, NI, NI), 0.12, 0.25, 0.04).astype(jnp.bfloat16)


def draw_coarse_inverse(key, part):
    key = jax.random.fold_in(key, 13)
    return spd_blocks(key, (GROUPS, MEMBERS, CROWS, CROWS), 1.0, 2.0, 0.4)


def draw_partners(key, part):
    key = jax.random.fold_in(key, 14)
    rounds = MEMBERS - 1
    tile_cap = (NT + MEMBERS - 2) // (MEMBERS - 1)

    def one_group(group_key):
        first_key, second_key = jax.random.split(group_key)
        sequence = jax.random.permutation(first_key, rounds * tile_cap)[:NT] % rounds
        orders = jax.vmap(lambda member_key: jax.random.permutation(member_key, NT))(jax.random.split(second_key, MEMBERS))
        member = jnp.arange(MEMBERS, dtype=jnp.int32)[:, None]
        round_id = sequence[orders].astype(jnp.int32)
        opposite = (2 * round_id - member) % rounds
        peer_dev = jnp.where(member == MEMBERS - 1, round_id, jnp.where(member == round_id, MEMBERS - 1, opposite))
        return jnp.stack([peer_dev, orders.astype(jnp.int32)], axis=1)
    group_keys = jax.random.split(key, GROUPS)
    return jax.vmap(one_group)(group_keys).astype(jnp.int32)


def touch_ends(array, own_key, least, high):
    extent = array.shape
    place = [jax.random.randint(jax.random.fold_in(own_key, axis), (), 0, extent[axis]) for axis in range(len(extent))]
    array = array.at[tuple(place)].set(least)
    longest = extent.index(max(extent))
    place[longest] = (place[longest] + 1) % extent[longest]
    return array.at[tuple(place)].set(high)


def level_of(key, extent, cuts, low, high):
    def one(dim, shards_of):
        draws = jax.random.uniform(jax.random.fold_in(jax.random.fold_in(key, 6), dim), (shards_of,), jnp.float32, low / len(cuts), high / len(cuts))
        return jnp.repeat(jnp.exp(draws), extent[dim] // shards_of).reshape((-1,) + (1,) * (len(extent) - dim - 1))

    level = one(*cuts[0])
    for cut in cuts[1:]:
        level = level * one(*cut)
    return level


def shared_out(key, own, number, rows, count, top, bound, skew):
    ranking = jax.random.permutation(key, count)
    crowded, ordinary = load_shares(count, rows * top, bound, skew, True), load_shares(count, rows * top, bound, skew, False)
    places = jnp.arange(count)

    def named(lengths, rotation):
        used = int((lengths > 0).sum())
        fixed = max(1, used // 4)
        passed = fixed + (places - fixed + rotation * (used - fixed)) % max(1, count - fixed)
        return jnp.zeros((count,), jnp.int32).at[ranking[jnp.where(places < fixed, places, passed)]].set(jnp.asarray(lengths, jnp.int32))

    lengths = jnp.where(number % 4 == 0, named(crowded, number // 4), named(ordinary, number - number // 4 - 1))
    mixed = jax.random.permutation(jax.random.fold_in(own, 3), count)
    giver, sink = mixed[0:count // 2 * 2:2], mixed[1:count // 2 * 2:2]
    margin = jnp.minimum(lengths[giver] - 1, bound - lengths[sink]) // 2
    margin = jnp.where((giver == ranking[0]) | (sink == ranking[0]) | (lengths[sink] == 0), 0, jnp.maximum(margin, 0))
    passed = jax.random.randint(jax.random.fold_in(own, 4), (count // 2,), 0, 1 << 20) % (margin + 1)
    lengths = lengths.at[giver].add(-passed).at[sink].add(passed)
    items = jnp.searchsorted(jnp.cumsum(lengths), jnp.arange(rows * top), side="right").astype(jnp.int32)
    listing = items.reshape(top, rows).T
    listing = listing[jax.random.permutation(jax.random.fold_in(own, 1), rows)]
    rotation = jax.random.randint(jax.random.fold_in(own, 2), (rows, 1), 0, top)
    return jnp.take_along_axis(listing, (jnp.arange(top)[None, :] + rotation) % top, axis=1)


def load_shares(number_of, total, most, slope, full):
    weights = [(1 << 20) // math.isqrt(standing ** slope) + 1 for standing in range(1, number_of + 1)]
    largest = most if full else min(most, max(-(-total // number_of), total * weights[0] // sum(weights)))
    least = 1 if total - largest >= number_of - 1 else 0
    counts, rest = [largest] + [least] * (number_of - 1), total - largest - least * (number_of - 1)
    while rest > 0:
        free = [i for i in range(1, number_of) if counts[i] < largest] or [i for i in range(1, number_of) if counts[i] < most]
        whole, budget = sum([weights[i] for i in free]), rest
        for i in free:
            more = min(most - counts[i], max(1, budget * weights[i] // whole), rest)
            counts[i] = counts[i] + more
            rest = rest - more
    return np.array(counts)


def normal_values(rng, shape, width, limit, cuts=(), held_as=jnp.bfloat16):
    gain = level_of(rng, shape, cuts, -0.22, 0.18) if cuts else 1.0
    drawn = jax.random.normal(rng, shape, jnp.float32) * width * gain
    return jnp.minimum(jnp.maximum(drawn, -limit), limit).astype(held_as)


def setup_inputs(seed: int = 0) -> dict:
    arg_keys = jax.random.split(jax.random.key(seed), 11)
    loads = normal_values(arg_keys[0], (GROUPS, MEMBERS, NI, K), 1.0, 6.0, ((0, 64), (1, 16)), jnp.float32)
    coefficient = jnp.clip(jnp.exp(math.log(4.0) - 2.0794415 * jax.random.uniform(arg_keys[1], (GROUPS, MEMBERS), jnp.float32) ** level_of(arg_keys[1], (GROUPS, MEMBERS), ((0, 64), (1, 16)), -0.2, 0.2)), 0.5, 4.0)
    schur_ref = draw_schur_ref(jax.random.fold_in(arg_keys[10], 71), 0)
    schur_inverse = draw_schur_inverse(jax.random.fold_in(arg_keys[10], 71), 0)
    coarse_basis = normal_values(arg_keys[4], (GROUPS, MEMBERS, NI, PMAX), NI ** -0.5, 0.1875, ((0, 64), (1, 16)))
    partners = draw_partners(jax.random.fold_in(arg_keys[10], 71), 0)
    routes_keys = jax.random.split(jax.random.fold_in(arg_keys[6], 1), GROUPS * MEMBERS * PMAX // PMAX)
    routes_turns = jax.random.permutation(jax.random.fold_in(arg_keys[6], 3), GROUPS * MEMBERS * PMAX // PMAX)
    routes = jax.vmap(lambda own, number: shared_out(jax.random.fold_in(arg_keys[6], 2), own, number, PMAX, GROUPS, 1, PCAP, 2))(routes_keys, routes_turns).reshape((GROUPS, MEMBERS, PMAX, 1))
    coarse_rows = touch_ends(jax.random.randint(arg_keys[7], (GROUPS, MEMBERS, PMAX), 0, CROWS), jax.random.fold_in(arg_keys[7], 1), 0, CROWS - 1).astype(jnp.int32)
    primal_count = touch_ends(jax.random.randint(arg_keys[8], (GROUPS, MEMBERS), PMAX // 2, PMAX + 1), jax.random.fold_in(arg_keys[8], 1), PMAX // 2, PMAX).astype(jnp.int32)
    coarse_inverse = draw_coarse_inverse(jax.random.fold_in(arg_keys[10], 71), 0)
    return {"loads": loads, "coefficient": coefficient, "schur_ref": schur_ref, "schur_inverse": schur_inverse, "coarse_basis": coarse_basis, "partners": partners, "routes": routes, "coarse_rows": coarse_rows, "primal_count": primal_count, "coarse_inverse": coarse_inverse}


exact_mode = lax.Precision.HIGHEST


def partner_rows(partners):
    peer_dev = partners[:, :, 0, :]
    pair_id = partners[:, :, 1, :]

    def one_group(peer_group, pair_group):
        their_peer = peer_group[peer_group]
        their_pair = pair_group[peer_group]
        member = jnp.arange(peer_group.shape[0], dtype=jnp.int32)[:, None, None]
        matched = (their_peer == member) & (their_pair == pair_group[:, :, None])
        position = jnp.argmax(matched.astype(jnp.int32), axis=2).astype(jnp.int32)
        return peer_group * peer_group.shape[1] + position

    return jax.vmap(one_group)(peer_dev, pair_id)


def reference(loads, coefficient, schur_ref, schur_inverse, coarse_basis, partners, routes, coarse_rows, primal_count, coarse_inverse):
    flat_partner = partner_rows(partners).reshape(GROUPS, MEMBERS * NT)
    live_rows = (jnp.arange(PMAX, dtype=jnp.int32)[None, None, :] < primal_count[:, :, None]).astype(jnp.float32)
    target = routes[:, :, :, 0]
    coarse_index = target * CROWS + coarse_rows
    member_ids = jnp.arange(MEMBERS, dtype=jnp.int32)[None, :, None]
    ref_wide = schur_ref.astype(jnp.float32)

    def assemble(vector):
        blocks = vector.reshape(GROUPS, MEMBERS * NT, TILE, K)
        mirrored = jax.vmap(lambda block_set, index_set: block_set[index_set])(blocks, flat_partner)
        return vector + mirrored.reshape(GROUPS, MEMBERS, NI, K)

    def to_narrow(vector):
        return lax.optimization_barrier(vector.astype(jnp.bfloat16)).astype(jnp.float32)

    def operate(vector):
        def one_group(group_args):
            group_vec, group_coef = group_args
            product = jnp.einsum('ij,mjk->mik', ref_wide, to_narrow(group_vec), precision=exact_mode)
            return group_coef[:, None, None] * product
        return assemble(lax.map(one_group, (vector, coefficient)))

    def precondition(residual):
        def one_group(group_args):
            inverse_group, basis_group, group_res = group_args
            local_part = 0.25 * jnp.einsum('mij,mjk->mik', inverse_group.astype(jnp.float32), to_narrow(group_res), precision=exact_mode)
            primal = jnp.einsum('mip,mik->mpk', basis_group.astype(jnp.float32), 0.5 * group_res, precision=exact_mode)
            return local_part, primal
        local_part, primal = lax.map(one_group, (schur_inverse, coarse_basis, residual))
        primal = primal * live_rows[..., None]

        def per_member(member_vals, member_index):
            return jax.ops.segment_sum(member_vals.reshape(GROUPS * PMAX, K), member_index.reshape(GROUPS * PMAX), num_segments=GROUPS * CROWS)

        coarse = jax.vmap(per_member, in_axes=(1, 1), out_axes=1)(primal, coarse_index)
        coarse = coarse.reshape(GROUPS, CROWS, MEMBERS, K).transpose(0, 2, 1, 3)
        solved = jnp.einsum('gmab,gmbk->gmak', coarse_inverse, coarse, precision=exact_mode)
        picked = solved[target, member_ids, coarse_rows] * live_rows[..., None]

        def lift_group(group_args):
            return jnp.einsum('mip,mpk->mik', group_args[0].astype(jnp.float32), group_args[1], precision=exact_mode)

        lifted = lax.map(lift_group, (coarse_basis, picked))
        return assemble(local_part + lifted)

    def column_dot(left, right):
        return 0.5 * jnp.sum(left * right, axis=(0, 1, 2))

    residual = assemble(loads)
    precond = precondition(residual)
    direction = precond
    energy = column_dot(residual, precond)
    solution = jnp.zeros_like(loads)
    for iteration in range(ITERS):
        applied = operate(direction)
        step_size = energy / column_dot(direction, applied)
        solution = solution + step_size * direction
        if iteration + 1 < ITERS:
            residual = residual - step_size * applied
            precond = precondition(residual)
            renewed = column_dot(residual, precond)
            direction = precond + (renewed / energy) * direction
            energy = renewed
    return solution
```

```python
import jax
import jax.numpy as jnp
from jax import lax
from jax.sharding import PartitionSpec as P

TILE = 128


def two_parts(value):
    high = lax.reduce_precision(value, 8, 7)
    low = value - high
    return jnp.concatenate([high, low], axis=1).astype(jnp.bfloat16)


def product(matrix, value, transposed=False):
    columns = value.shape[1]
    contract = ((0,), (0,)) if transposed else ((1,), (0,))
    both = lax.dot_general(
        matrix, two_parts(value), (contract, ((), ())), preferred_element_type=jnp.float32
    )
    return both[:, :columns] + both[:, columns:]


def body(
    loads,
    coefficient,
    schur_ref,
    schur_inverse,
    coarse_basis,
    partners,
    routes,
    coarse_rows,
    primal_count,
    coarse_inverse,
):
    rows_total = loads.shape[2]
    columns = loads.shape[3]
    peer_dev = partners[0, 0, 0]
    tile_count = peer_dev.shape[0]
    tile = rows_total // tile_count
    members = lax.axis_size("dom")
    groups = lax.axis_size("sub")
    primal_max = coarse_basis.shape[3]
    primal_cap = max(2, (primal_max + groups - 1) // groups)
    slots = groups * primal_cap
    coarse_size = coarse_inverse.shape[3]

    slot_match = jnp.arange(members, dtype=jnp.int32)[:, None] == peer_dev[None, :]
    tile_ids = jnp.arange(tile_count, dtype=jnp.int32)
    slot_source = jnp.sum(jnp.where(slot_match, tile_ids[None, :], 0), axis=1)

    def assemble(vector):
        tiles = vector.reshape(tile_count, tile, columns)
        incoming = lax.all_to_all(tiles[slot_source], "dom", 0, 0, tiled=True)
        return vector + incoming[peer_dev].reshape(rows_total, columns)

    primal_pos = jnp.arange(primal_max, dtype=jnp.int32)
    live = primal_pos < primal_count[0, 0]
    target = routes[0, 0, :, 0]
    ahead = (target[None, :] == target[:, None]) & (primal_pos[None, :] < primal_pos[:, None])
    primal_slot = target * primal_cap + jnp.sum(ahead.astype(jnp.int32), axis=1)
    send_mask = jnp.arange(slots, dtype=jnp.int32)[:, None] == primal_slot[None, :]
    send_mask = send_mask & live[None, :]
    labels = jnp.sum(jnp.where(send_mask, coarse_rows[0, 0][None, :] + 1, 0), axis=1)
    slot_basis = lax.dot_general(
        coarse_basis[0, 0],
        send_mask.astype(jnp.bfloat16),
        (((1,), (1,)), ((), ())),
        preferred_element_type=jnp.float32,
    ).astype(jnp.bfloat16)
    label_rows = jnp.pad(
        labels.reshape(groups, 1, primal_cap).astype(jnp.float32),
        ((0, 0), (0, 0), (0, columns - primal_cap)),
    )
    inverse_local = schur_inverse[0, 0]
    stiffness = coefficient[0, 0]
    coarse_ids = jnp.arange(coarse_size, dtype=jnp.int32).astype(jnp.float32)
    exact = lax.Precision.HIGHEST

    def shift(values):
        return lax.all_to_all(values, "sub", 0, 0, tiled=True)

    def primal_of(residual):
        return product(slot_basis, 0.5 * residual, True).reshape(groups, primal_cap, columns)

    def lifted(answer, residual):
        returned = shift(answer.reshape(groups, primal_cap, columns)).reshape(slots, columns)
        return 0.25 * product(inverse_local, residual) + product(slot_basis, returned)

    residual = assemble(loads[0, 0])
    arrived = shift(jnp.concatenate([primal_of(residual), label_rows], axis=1))
    labels_in = arrived[:, primal_cap, :primal_cap].reshape(slots)
    owner = (labels_in[:, None] - 1.0 == coarse_ids[None, :]).astype(jnp.float32)
    coupling = jnp.dot(
        jnp.dot(owner, coarse_inverse[0, 0], precision=exact), owner.T, precision=exact
    )
    values = arrived[:, :primal_cap].reshape(slots, columns)
    half_first = lifted(jnp.dot(coupling, values, precision=exact), residual)
    first = assemble(half_first)
    energy = jnp.sum(residual * half_first, axis=0)

    half_image = stiffness * product(schur_ref, first)
    image = assemble(half_image)
    gram_first = jnp.sum(first * half_image, axis=0)
    values = shift(primal_of(image)).reshape(slots, columns)
    half_second = lifted(jnp.dot(coupling, values, precision=exact), image)
    second = assemble(half_second)
    gram_mixed = jnp.sum(image * half_second, axis=0)
    gram_second = stiffness * jnp.sum(second * product(schur_ref, second), axis=0)

    sums = jnp.stack([energy, gram_first, gram_mixed, gram_second])
    sums = jnp.sum(shift(jnp.broadcast_to(sums[None], (groups, 4, columns))), axis=0)
    spread = jnp.broadcast_to(sums[None], (members, 4, columns))
    sums = jnp.sum(lax.all_to_all(spread, "dom", 0, 0, tiled=True), axis=0)
    energy, gram_first, gram_mixed, gram_second = sums[0], sums[1], sums[2], sums[3]

    step_first = energy / gram_first
    mixed_share = gram_mixed / gram_first
    step_second = (gram_mixed - gram_first / energy * gram_first) / (
        gram_second - mixed_share * gram_mixed
    )
    along_first = step_first + step_second * (step_first * mixed_share)
    along_second = step_second * step_first
    solution = along_first * first - along_second * second
    return solution.reshape(1, 1, rows_total, columns)


def solution(mesh):
    return jax.shard_map(
        body,
        mesh=mesh,
        in_specs=(
            P("sub", "dom", None, None),
            P("sub", "dom"),
            P(),
            P("sub", "dom", None, None),
            P("sub", "dom", None, None),
            P("sub", "dom", None, None),
            P("sub", "dom", None, None),
            P("sub", "dom", None),
            P("sub", "dom"),
            P("sub", "dom", None, None),
        ),
        out_specs=P("sub", "dom", None, None),
        check_vma=False,
    )
```

```python
import functools

import jax
import jax.numpy as jnp
from jax import lax
from jax.experimental import pallas as pl
from jax.experimental.pallas import tpu as pltpu
from jax.sharding import PartitionSpec as P

F32 = jnp.float32
BF16 = jnp.bfloat16
VMEM = pl.BlockSpec(memory_space=pltpu.VMEM)
SMEM = pl.BlockSpec(memory_space=pltpu.SMEM)


def parts_of(value):
    high = value.astype(BF16)
    low = (value - high.astype(F32)).astype(BF16)
    return high, low


def dot(left, right):
    return jnp.dot(left, right, preferred_element_type=F32)


def product(matrix, value):
    columns = value.shape[1]
    both = dot(matrix, jnp.concatenate(parts_of(value), axis=1))
    return both[:, :columns] + both[:, columns:]


def spread(peers_ref, value, out_ref):
    tile = out_ref.shape[1]
    out_ref[...] = jnp.zeros_like(out_ref)
    for t in range(value.shape[0] // tile):
        out_ref[peers_ref[0, t]] = value[t * tile : (t + 1) * tile]


def mirrored(peers_ref, half_ref, incoming_ref, out_ref):
    tile = incoming_ref.shape[1]
    for t in range(half_ref.shape[0] // tile):
        rows = slice(t * tile, (t + 1) * tile)
        out_ref[rows] = half_ref[rows] + incoming_ref[peers_ref[0, t]]


def column_sum(value):
    return jnp.sum(value, axis=0, keepdims=True)


def send_loads_kernel(peers_ref, loads_ref, out_ref):
    spread(peers_ref, loads_ref[...], out_ref)


def first_residual_kernel(peers_ref, loads_ref, incoming_ref, basis_ref, labels_ref, residual_ref, out_ref):
    mirrored(peers_ref, loads_ref, incoming_ref, residual_ref)
    out_ref[...] = product(basis_ref[...], 0.5 * residual_ref[...]) + labels_ref[...]


def residual_kernel(peers_ref, half_ref, incoming_ref, basis_ref, residual_ref, out_ref):
    mirrored(peers_ref, half_ref, incoming_ref, residual_ref)
    out_ref[...] = product(basis_ref[...], 0.5 * residual_ref[...])


def local_kernel(inverse_ref, residual_ref, out_ref):
    out_ref[...] = 0.25 * product(inverse_ref[...], residual_ref[...])


def split_product(high, low, value):
    value_high, value_low = parts_of(value)
    return dot(
        jnp.concatenate([high, high, low], axis=1),
        jnp.concatenate([value_high, value_low, value_high], axis=0),
    )


def first_coarse_kernel(cap, stride, arrived_ref, block_ref, high_ref, low_ref, out_ref):
    slots, columns = out_ref.shape
    coarse_size = block_ref.shape[0]
    received = arrived_ref.shape[0]
    arrived = jnp.concatenate(parts_of(arrived_ref[...]), axis=1)
    slot = lax.broadcasted_iota(jnp.int32, (slots, received), 0)
    row = lax.broadcasted_iota(jnp.int32, (slots, received), 1)
    base = (slot // cap) * stride
    pick_value = (row == base + slot % cap).astype(F32).astype(BF16)
    pick_label = (row == base + cap).astype(F32).astype(BF16)
    values = dot(pick_value, arrived)
    values = values[:, :columns] + values[:, columns:]
    label_rows = dot(pick_label, arrived[:, :columns])
    lane = lax.broadcasted_iota(jnp.int32, (slots, columns), 1)
    own = lax.broadcasted_iota(jnp.int32, (slots, columns), 0) % cap
    labels = jnp.sum(jnp.where(lane == own, label_rows, 0.0), axis=1, keepdims=True)
    ids = lax.broadcasted_iota(jnp.int32, (slots, coarse_size), 1).astype(F32)
    owner = (labels - 1.0 == ids).astype(F32).astype(BF16)
    block_high, block_low = parts_of(block_ref[...])
    across = (((1,), (1,)), ((), ()))

    def composed(part):
        rows = dot(owner, part).astype(BF16)
        return lax.dot_general(rows, owner, across, preferred_element_type=F32).astype(BF16)

    high, low = composed(block_high), composed(block_low)
    high_ref[...] = high
    low_ref[...] = low
    out_ref[...] = split_product(high, low, values)


def coarse_kernel(high_ref, low_ref, values_ref, out_ref):
    out_ref[...] = split_product(high_ref[...], low_ref[...], values_ref[...])


def lift_kernel(peers_ref, basis_ref, returned_ref, local_ref, residual_ref, half_ref, out_ref, sum_ref):
    half = local_ref[...] + product(basis_ref[...], returned_ref[...])
    half_ref[...] = half
    spread(peers_ref, half, out_ref)
    sum_ref[...] = column_sum(residual_ref[...] * half)


def operate_kernel(peers_ref, stiffness_ref, half_ref, incoming_ref, schur_ref, vector_ref, image_ref, out_ref, sum_ref):
    mirrored(peers_ref, half_ref, incoming_ref, vector_ref)
    vector = vector_ref[...]
    image = stiffness_ref[0, 0] * product(schur_ref[...], vector)
    image_ref[...] = image
    spread(peers_ref, image, out_ref)
    sum_ref[...] = column_sum(vector * image)


def last_kernel(
    peers_ref, stiffness_ref, half_ref, incoming_ref, schur_ref, energy_ref, first_ref, mixed_ref, vector_ref, out_ref
):
    mirrored(peers_ref, half_ref, incoming_ref, vector_ref)
    vector = vector_ref[...]
    second = stiffness_ref[0, 0] * column_sum(vector * product(schur_ref[...], vector))
    sums = jnp.concatenate([energy_ref[...], first_ref[...], mixed_ref[...], second], axis=0)
    out_ref[...] = jnp.broadcast_to(sums[None], out_ref.shape)


def regroup_kernel(sums_ref, out_ref):
    out_ref[...] = jnp.broadcast_to(jnp.sum(sums_ref[...], axis=0)[None], out_ref.shape)


def combine_kernel(sums_ref, first_ref, second_ref, out_ref):
    sums = jnp.sum(sums_ref[...], axis=0)
    energy, gram_first, gram_mixed, gram_second = (sums[i : i + 1] for i in range(4))
    step_first = energy / gram_first
    mixed_share = gram_mixed / gram_first
    step_second = (gram_mixed - gram_first / energy * gram_first) / (
        gram_second - mixed_share * gram_mixed
    )
    along_first = step_first + step_second * (step_first * mixed_share)
    along_second = step_second * step_first
    out_ref[...] = along_first * first_ref[...] - along_second * second_ref[...]


def call(kernel, scalars, inputs, outputs, flops=0):
    moved = sum(x.size * x.dtype.itemsize for x in inputs)
    moved += sum(x.size * x.dtype.itemsize for x in outputs)
    single = len(outputs) == 1
    return pl.pallas_call(
        kernel,
        out_shape=outputs[0] if single else tuple(outputs),
        in_specs=[SMEM] * len(scalars) + [VMEM] * len(inputs),
        out_specs=VMEM if single else tuple([VMEM] * len(outputs)),
        compiler_params=pltpu.CompilerParams(vmem_limit_bytes=20 << 20),
        cost_estimate=pl.CostEstimate(flops=flops, bytes_accessed=moved, transcendentals=0),
    )(*scalars, *inputs)


def body(
    loads,
    coefficient,
    schur_ref,
    schur_inverse,
    coarse_basis,
    partners,
    routes,
    coarse_rows,
    primal_count,
    coarse_inverse,
):
    rows_total, columns = loads.shape[2:]
    peers = partners[0, 0]
    tile_count = peers.shape[1]
    tile = rows_total // tile_count
    members = lax.axis_size("dom")
    groups = lax.axis_size("sub")
    primal_max = coarse_basis.shape[3]
    cap = max(2, (primal_max + groups - 1) // groups)
    stride = cap + 1
    slots = groups * cap
    stiffness = coefficient
    load_tiles = loads[0, 0]
    inverse_local = schur_inverse[0, 0]

    def shaped(*shape, dtype=F32):
        return jax.ShapeDtypeStruct(shape, dtype)

    vector_shape = shaped(rows_total, columns)
    slot_shape = shaped(slots, columns)
    tiles_shape = shaped(members, tile, columns)
    sum_shape = shaped(1, columns)
    big = 4 * rows_total * rows_total * columns
    thin = 4 * rows_total * slots * columns

    def exchange(tiles):
        return lax.all_to_all(tiles, "dom", 0, 0, tiled=True)

    def shift(values, per_group):
        grouped = values.reshape(groups, 1, per_group * columns)
        return lax.all_to_all(grouped, "sub", 0, 0, tiled=True).reshape(groups * per_group, columns)

    cores = 2
    chips = groups // cores
    layers = [
        [(z * cores + k) * members + d for k in range(cores) for d in range(members)]
        for z in range(chips)
    ]
    lines = [list(line) for line in zip(*layers)]

    def gather(values, sets):
        return lax.all_to_all(values, ("sub", "dom"), 0, 0, tiled=True, axis_index_groups=sets)

    incoming = exchange(call(send_loads_kernel, [peers], [load_tiles], [tiles_shape]))

    primal_pos = jnp.arange(primal_max, dtype=jnp.int32)
    live = primal_pos < primal_count[0, 0]
    target = routes[0, 0, :, 0]
    ahead = (target[None, :] == target[:, None]) & (primal_pos[None, :] < primal_pos[:, None])
    rank = jnp.sum(ahead.astype(jnp.int32), axis=1)
    basis = coarse_basis[0, 0]

    def placed(per_group):
        wanted = jnp.where(live, target * per_group + rank, -1)
        return jnp.arange(groups * per_group, dtype=jnp.int32)[:, None] == wanted[None, :]

    def chosen(per_group, basis_first):
        table = placed(per_group).astype(BF16)
        pair = (basis, table) if basis_first else (table, basis)
        across = (((1,), (1,)), ((), ()))
        return lax.dot_general(*pair, across, preferred_element_type=F32).astype(BF16)

    row_labels = jnp.where(live, coarse_rows[0, 0] + 1, 0)
    labels = jnp.sum(jnp.where(placed(cap), row_labels[None, :], 0), axis=1)
    labels = jnp.pad(labels.reshape(groups, 1, cap), ((0, 0), (cap, stride - cap - 1), (0, columns - cap)))
    labels = labels.reshape(groups * stride, columns).astype(F32)
    lift_basis = chosen(cap, True)
    slot_basis = chosen(cap, False)
    wide_basis = chosen(stride, False)

    residual, outgoing = call(
        first_residual_kernel,
        [peers],
        [load_tiles, incoming, wide_basis, labels],
        [vector_shape, shaped(groups * stride, columns)],
        2 * thin,
    )
    arrived = shift(outgoing, stride)
    local = call(local_kernel, [], [inverse_local, residual], [vector_shape], big)
    high, low, answer = call(
        functools.partial(first_coarse_kernel, cap, stride),
        [],
        [arrived, coarse_inverse[0, 0]],
        [shaped(slots, slots, dtype=BF16), shaped(slots, slots, dtype=BF16), slot_shape],
        20 * slots * slots * columns,
    )
    returned = shift(answer, cap)
    half, tiles, energy = call(
        lift_kernel,
        [peers],
        [lift_basis, returned, local, residual],
        [vector_shape, tiles_shape, sum_shape],
        thin,
    )
    incoming = exchange(tiles)
    first, half, tiles, gram_first = call(
        operate_kernel,
        [peers, stiffness],
        [half, incoming, schur_ref],
        [vector_shape, vector_shape, tiles_shape, sum_shape],
        big,
    )
    incoming = exchange(tiles)
    image, outgoing = call(
        residual_kernel, [peers], [half, incoming, slot_basis], [vector_shape, slot_shape], thin
    )
    arrived = shift(outgoing, cap)
    local = call(local_kernel, [], [inverse_local, image], [vector_shape], big)
    answer = call(coarse_kernel, [], [high, low, arrived], [slot_shape], 6 * slots * slots * columns)
    returned = shift(answer, cap)
    half, tiles, gram_mixed = call(
        lift_kernel,
        [peers],
        [lift_basis, returned, local, image],
        [vector_shape, tiles_shape, sum_shape],
        thin,
    )
    incoming = exchange(tiles)
    second, sums = call(
        last_kernel,
        [peers, stiffness],
        [half, incoming, schur_ref, energy, gram_first, gram_mixed],
        [vector_shape, shaped(cores * members, 4, columns)],
        big,
    )
    sums = call(regroup_kernel, [], [gather(sums, layers)], [shaped(chips, 4, columns)])
    sums = gather(sums, lines)
    solution = call(combine_kernel, [], [sums, first, second], [vector_shape])
    return solution.reshape(1, 1, rows_total, columns)


def solution(mesh):
    return jax.shard_map(
        body,
        mesh=mesh,
        in_specs=(
            P("sub", "dom", None, None),
            P("sub", "dom"),
            P(),
            P("sub", "dom", None, None),
            P("sub", "dom", None, None),
            P("sub", "dom", None, None),
            P("sub", "dom", None, None),
            P("sub", "dom", None),
            P("sub", "dom"),
            P("sub", "dom", None, None),
        ),
        out_specs=P("sub", "dom", None, None),
        check_vma=False,
    )
```

```python
import functools

import jax
import jax.numpy as jnp
from jax import lax
from jax.experimental import pallas as pl
from jax.experimental.pallas import tpu as pltpu
from jax.sharding import PartitionSpec as P

F32 = jnp.float32
BF16 = jnp.bfloat16
VMEM = pl.BlockSpec(memory_space=pltpu.VMEM)
SMEM = pl.BlockSpec(memory_space=pltpu.SMEM)


def parts_of(value):
    high = value.astype(BF16)
    low = (value - high.astype(F32)).astype(BF16)
    return high, low


def dot(left, right):
    return jnp.dot(left, right, preferred_element_type=F32)


def product(matrix, value):
    columns = value.shape[1]
    both = dot(matrix, jnp.concatenate(parts_of(value), axis=1))
    return both[:, :columns] + both[:, columns:]


def spread(peers_ref, value, out_ref):
    tile = out_ref.shape[1]
    out_ref[...] = jnp.zeros_like(out_ref)
    for t in range(value.shape[0] // tile):
        out_ref[peers_ref[0, t]] = value[t * tile : (t + 1) * tile]


def mirrored(peers_ref, half_ref, incoming_ref, out_ref):
    tile = incoming_ref.shape[1]
    for t in range(half_ref.shape[0] // tile):
        rows = slice(t * tile, (t + 1) * tile)
        out_ref[rows] = half_ref[rows] + incoming_ref[peers_ref[0, t]]


def column_sum(value):
    return jnp.sum(value, axis=0, keepdims=True)


def send_loads_kernel(
    cap,
    peers_ref,
    count_ref,
    stiffness_ref,
    loads_ref,
    basis_ref,
    routes_ref,
    rows_ref,
    out_ref,
    slot_basis_ref,
    wide_basis_ref,
    lift_basis_ref,
    labels_ref,
    scale_ref,
):
    spread(peers_ref, loads_ref[...], out_ref)
    scale_ref[...] = jnp.full_like(scale_ref, stiffness_ref[0, 0])
    target = routes_ref[...]
    listed = target.shape[1]
    first = lax.broadcasted_iota(jnp.int32, (listed, listed), 0)
    second = lax.broadcasted_iota(jnp.int32, (listed, listed), 1)
    column = jnp.sum(jnp.where(first == second, target, 0), axis=1, keepdims=True)
    ahead = jnp.where(first < second, 1, 0) * jnp.where(column == target, 1, 0)
    rank = jnp.sum(ahead, axis=0, keepdims=True)
    live = lax.broadcasted_iota(jnp.int32, target.shape, 1) < count_ref[0, 0]
    slot = jnp.where(live, target * cap + rank, -1)
    wide_slot = jnp.where(live, target * (cap + 1) + rank, -1)
    basis = basis_ref[...]

    def table_of(count, wanted):
        index = lax.broadcasted_iota(jnp.int32, (count, listed), 0)
        return jnp.where(index == wanted, 1.0, 0.0).astype(BF16)

    slot_table = table_of(slot_basis_ref.shape[0], slot)
    slot_basis = dot(slot_table, basis)
    slot_basis_ref[...] = slot_basis.astype(BF16)
    lift_basis_ref[...] = jnp.transpose(slot_basis).astype(BF16)
    wide_basis_ref[...] = dot(table_of(wide_basis_ref.shape[0], wide_slot), basis).astype(BF16)
    label = jnp.where(live, rows_ref[...] + 1, 0)
    lane = lax.broadcasted_iota(jnp.int32, labels_ref.shape, 1)
    index = lax.broadcasted_iota(jnp.int32, (labels_ref.shape[0], listed), 0)
    labels = jnp.zeros(labels_ref.shape, F32)
    for i in range(cap):
        wanted = jnp.where(rank == i, target * (cap + 1) + cap, -1)
        found = jnp.sum(jnp.where(index == wanted, label, 0), axis=1, keepdims=True)
        labels = jnp.where(lane == i, found.astype(F32), labels)
    labels_ref[...] = labels


def first_residual_kernel(peers_ref, loads_ref, incoming_ref, basis_ref, labels_ref, residual_ref, out_ref):
    mirrored(peers_ref, loads_ref, incoming_ref, residual_ref)
    out_ref[...] = product(basis_ref[...], 0.5 * residual_ref[...]) + labels_ref[...]


def residual_kernel(peers_ref, half_ref, incoming_ref, basis_ref, residual_ref, out_ref):
    mirrored(peers_ref, half_ref, incoming_ref, residual_ref)
    out_ref[...] = product(basis_ref[...], 0.5 * residual_ref[...])


def split_product(high, low, value):
    value_high, value_low = parts_of(value)
    return dot(
        jnp.concatenate([high, high, low], axis=1),
        jnp.concatenate([value_high, value_low, value_high], axis=0),
    )


def first_coarse_kernel(cap, stride, arrived_ref, block_ref, high_ref, low_ref, out_ref):
    slots, columns = out_ref.shape
    coarse_size = block_ref.shape[0]
    received = arrived_ref.shape[0]
    arrived = jnp.concatenate(parts_of(arrived_ref[...]), axis=1)
    slot = lax.broadcasted_iota(jnp.int32, (slots, received), 0)
    row = lax.broadcasted_iota(jnp.int32, (slots, received), 1)
    base = (slot // cap) * stride
    pick_value = (row == base + slot % cap).astype(F32).astype(BF16)
    pick_label = (row == base + cap).astype(F32).astype(BF16)
    values = dot(pick_value, arrived)
    values = values[:, :columns] + values[:, columns:]
    label_rows = dot(pick_label, arrived[:, :columns])
    lane = lax.broadcasted_iota(jnp.int32, (slots, columns), 1)
    own = lax.broadcasted_iota(jnp.int32, (slots, columns), 0) % cap
    labels = jnp.sum(jnp.where(lane == own, label_rows, 0.0), axis=1, keepdims=True)
    ids = lax.broadcasted_iota(jnp.int32, (slots, coarse_size), 1).astype(F32)
    owner = (labels - 1.0 == ids).astype(F32).astype(BF16)
    block_high, block_low = parts_of(block_ref[...])
    across = (((1,), (1,)), ((), ()))

    def composed(part):
        rows = dot(owner, part).astype(BF16)
        return lax.dot_general(rows, owner, across, preferred_element_type=F32).astype(BF16)

    high, low = composed(block_high), composed(block_low)
    high_ref[...] = high
    low_ref[...] = low
    out_ref[...] = split_product(high, low, values)


def coarse_kernel(high_ref, low_ref, values_ref, out_ref):
    out_ref[...] = split_product(high_ref[...], low_ref[...], values_ref[...])


def lift_kernel(
    peers_ref, inverse_ref, basis_ref, returned_ref, residual_ref, half_ref, out_ref, sum_ref
):
    residual = residual_ref[...]
    half = 0.25 * product(inverse_ref[...], residual) + product(basis_ref[...], returned_ref[...])
    half_ref[...] = half
    spread(peers_ref, half, out_ref)
    sum_ref[...] = column_sum(residual * half)


def operate_kernel(
    peers_ref, half_ref, incoming_ref, schur_ref, scale_ref, vector_ref, image_ref, out_ref, sum_ref
):
    mirrored(peers_ref, half_ref, incoming_ref, vector_ref)
    vector = vector_ref[...]
    image = scale_ref[...] * product(schur_ref[...], vector)
    image_ref[...] = image
    spread(peers_ref, image, out_ref)
    sum_ref[...] = column_sum(vector * image)


def last_kernel(
    peers_ref,
    half_ref,
    incoming_ref,
    schur_ref,
    scale_ref,
    energy_ref,
    first_ref,
    mixed_ref,
    vector_ref,
    out_ref,
):
    mirrored(peers_ref, half_ref, incoming_ref, vector_ref)
    vector = vector_ref[...]
    second = scale_ref[...] * column_sum(vector * product(schur_ref[...], vector))
    sums = jnp.concatenate([energy_ref[...], first_ref[...], mixed_ref[...], second], axis=0)
    out_ref[...] = jnp.broadcast_to(sums[None], out_ref.shape)


def regroup_kernel(sums_ref, out_ref):
    out_ref[...] = jnp.broadcast_to(jnp.sum(sums_ref[...], axis=0)[None], out_ref.shape)


def combine_kernel(sums_ref, first_ref, second_ref, out_ref):
    sums = jnp.sum(sums_ref[...], axis=0)
    energy, gram_first, gram_mixed, gram_second = (sums[i : i + 1] for i in range(4))
    step_first = energy / gram_first
    mixed_share = gram_mixed / gram_first
    step_second = (gram_mixed - gram_first / energy * gram_first) / (
        gram_second - mixed_share * gram_mixed
    )
    along_first = step_first + step_second * (step_first * mixed_share)
    along_second = step_second * step_first
    out_ref[...] = along_first * first_ref[...] - along_second * second_ref[...]


def call(kernel, scalars, inputs, outputs, flops=0):
    moved = sum(x.size * x.dtype.itemsize for x in inputs)
    moved += sum(x.size * x.dtype.itemsize for x in outputs)
    single = len(outputs) == 1
    return pl.pallas_call(
        kernel,
        out_shape=outputs[0] if single else tuple(outputs),
        in_specs=[SMEM] * len(scalars) + [VMEM] * len(inputs),
        out_specs=VMEM if single else tuple([VMEM] * len(outputs)),
        compiler_params=pltpu.CompilerParams(vmem_limit_bytes=20 << 20),
        cost_estimate=pl.CostEstimate(flops=flops, bytes_accessed=moved, transcendentals=0),
    )(*scalars, *inputs)


def body(
    loads,
    coefficient,
    schur_ref,
    schur_inverse,
    coarse_basis,
    partners,
    routes,
    coarse_rows,
    primal_count,
    coarse_inverse,
):
    rows_total, columns = loads.shape[2:]
    peers = partners[0, 0]
    tile_count = peers.shape[1]
    tile = rows_total // tile_count
    members = lax.axis_size("dom")
    groups = lax.axis_size("sub")
    primal_max = coarse_basis.shape[3]
    cap = max(2, (primal_max + groups - 1) // groups)
    stride = cap + 1
    slots = groups * cap
    load_tiles = loads[0, 0]
    inverse_local = schur_inverse[0, 0]

    def shaped(*shape, dtype=F32):
        return jax.ShapeDtypeStruct(shape, dtype)

    vector_shape = shaped(rows_total, columns)
    slot_shape = shaped(slots, columns)
    tiles_shape = shaped(members, tile, columns)
    sum_shape = shaped(1, columns)
    big = 4 * rows_total * rows_total * columns
    thin = 4 * rows_total * slots * columns

    def exchange(tiles):
        return lax.all_to_all(tiles, "dom", 0, 0, tiled=True)

    def shift(values, per_group):
        grouped = values.reshape(groups, 1, per_group * columns)
        return lax.all_to_all(grouped, "sub", 0, 0, tiled=True).reshape(groups * per_group, columns)

    cores = 2
    chips = groups // cores
    layers = [
        [(z * cores + k) * members + d for k in range(cores) for d in range(members)]
        for z in range(chips)
    ]
    lines = [list(line) for line in zip(*layers)]

    def gather(values, sets):
        return lax.all_to_all(values, ("sub", "dom"), 0, 0, tiled=True, axis_index_groups=sets)

    outgoing, slot_basis, wide_basis, lift_basis, labels, scale = call(
        functools.partial(send_loads_kernel, cap),
        [peers, primal_count, coefficient],
        [load_tiles, coarse_basis[0, 0].T, routes.reshape(1, primal_max), coarse_rows[0]],
        [
            tiles_shape,
            shaped(slots, rows_total, dtype=BF16),
            shaped(groups * stride, rows_total, dtype=BF16),
            shaped(rows_total, slots, dtype=BF16),
            shaped(groups * stride, columns),
            sum_shape,
        ],
        thin,
    )
    incoming = exchange(outgoing)
    residual, outgoing = call(
        first_residual_kernel,
        [peers],
        [load_tiles, incoming, wide_basis, labels],
        [vector_shape, shaped(groups * stride, columns)],
        2 * thin,
    )
    arrived = shift(outgoing, stride)
    high, low, answer = call(
        functools.partial(first_coarse_kernel, cap, stride),
        [],
        [arrived, coarse_inverse[0, 0]],
        [shaped(slots, slots, dtype=BF16), shaped(slots, slots, dtype=BF16), slot_shape],
        20 * slots * slots * columns,
    )
    returned = shift(answer, cap)
    half, tiles, energy = call(
        lift_kernel,
        [peers],
        [inverse_local, lift_basis, returned, residual],
        [vector_shape, tiles_shape, sum_shape],
        big + thin,
    )
    incoming = exchange(tiles)
    first, half, tiles, gram_first = call(
        operate_kernel,
        [peers],
        [half, incoming, schur_ref, scale],
        [vector_shape, vector_shape, tiles_shape, sum_shape],
        big,
    )
    incoming = exchange(tiles)
    image, outgoing = call(
        residual_kernel, [peers], [half, incoming, slot_basis], [vector_shape, slot_shape], thin
    )
    arrived = shift(outgoing, cap)
    answer = call(coarse_kernel, [], [high, low, arrived], [slot_shape], 6 * slots * slots * columns)
    returned = shift(answer, cap)
    half, tiles, gram_mixed = call(
        lift_kernel,
        [peers],
        [inverse_local, lift_basis, returned, image],
        [vector_shape, tiles_shape, sum_shape],
        big + thin,
    )
    incoming = exchange(tiles)
    second, sums = call(
        last_kernel,
        [peers],
        [half, incoming, schur_ref, scale, energy, gram_first, gram_mixed],
        [vector_shape, shaped(cores * members, 4, columns)],
        big,
    )
    sums = call(regroup_kernel, [], [gather(sums, layers)], [shaped(chips, 4, columns)])
    sums = gather(sums, lines)
    solution = call(combine_kernel, [], [sums, first, second], [vector_shape])
    return solution.reshape(1, 1, rows_total, columns)


def solution(mesh):
    return jax.shard_map(
        body,
        mesh=mesh,
        in_specs=(
            P("sub", "dom", None, None),
            P("sub", "dom"),
            P(),
            P("sub", "dom", None, None),
            P("sub", "dom", None, None),
            P("sub", "dom", None, None),
            P("sub", "dom", None, None),
            P("sub", "dom", None),
            P("sub", "dom"),
            P("sub", "dom", None, None),
        ),
        out_specs=P("sub", "dom", None, None),
        check_vma=False,
    )
```

```python
import functools
import math

import jax
import jax.numpy as jnp
from jax import lax
from jax.experimental import pallas as pl
from jax.experimental.pallas import tpu as pltpu
from jax.sharding import PartitionSpec as P

F32 = jnp.float32
BF16 = jnp.bfloat16
VMEM = pl.BlockSpec(memory_space=pltpu.VMEM)
SMEM = pl.BlockSpec(memory_space=pltpu.SMEM)


def parts_of(value):
    high = value.astype(BF16)
    low = (value - high.astype(F32)).astype(BF16)
    return high, low


def dot(left, right):
    return jnp.dot(left, right, preferred_element_type=F32)


def product(matrix, value):
    columns = value.shape[1]
    both = dot(matrix, jnp.concatenate(parts_of(value), axis=1))
    return both[:, :columns] + both[:, columns:]


def middle_of_plane(members):
    side = math.isqrt(members)
    return side // 2 * side + side // 2


def rotated(count, first):
    return [(first + i) % count for i in range(count)]


def place_of(peers_ref, t, members):
    return lax.rem(peers_ref[0, t] + (members - middle_of_plane(members)), members)


def spread(peers_ref, value, out_ref):
    members, tile = out_ref.shape[:2]
    out_ref[...] = jnp.zeros_like(out_ref)
    for t in range(value.shape[0] // tile):
        out_ref[place_of(peers_ref, t, members)] = value[t * tile : (t + 1) * tile]


def mirrored(peers_ref, half_ref, incoming_ref, out_ref):
    members, tile = incoming_ref.shape[:2]
    for t in range(half_ref.shape[0] // tile):
        rows = slice(t * tile, (t + 1) * tile)
        out_ref[rows] = half_ref[rows] + incoming_ref[place_of(peers_ref, t, members)]


def column_sum(value):
    return jnp.sum(value, axis=0, keepdims=True)


def first_kernel(
    cap,
    count_ref,
    stiffness_ref,
    peers_hbm,
    routes_hbm,
    rows_hbm,
    loads_hbm,
    basis_hbm,
    out_ref,
    slot_basis_ref,
    wide_basis_ref,
    lift_basis_ref,
    labels_ref,
    scale_ref,
    peers_ref,
    routes_ref,
    rows_ref,
    loads_ref,
    basis_ref,
    semaphores,
):
    sources = (peers_hbm, routes_hbm, rows_hbm, loads_hbm, basis_hbm)
    targets = (peers_ref, routes_ref, rows_ref, loads_ref, basis_ref)
    copies = [
        pltpu.make_async_copy(source, target, semaphores.at[i])
        for i, (source, target) in enumerate(zip(sources, targets))
    ]
    for copy in copies:
        copy.start()
    scale_ref[...] = jnp.full_like(scale_ref, stiffness_ref[0, 0])
    for copy in copies:
        copy.wait()
    spread(peers_ref, loads_ref[...], out_ref)
    groups = slot_basis_ref.shape[0] // cap
    target = lax.rem(routes_ref[...] + (groups - groups // 2), groups)
    listed = target.shape[1]
    first = lax.broadcasted_iota(jnp.int32, (listed, listed), 0)
    second = lax.broadcasted_iota(jnp.int32, (listed, listed), 1)
    column = jnp.sum(jnp.where(first == second, target, 0), axis=1, keepdims=True)
    ahead = jnp.where(first < second, 1, 0) * jnp.where(column == target, 1, 0)
    rank = jnp.sum(ahead, axis=0, keepdims=True)
    live = lax.broadcasted_iota(jnp.int32, target.shape, 1) < count_ref[0, 0]
    slot = jnp.where(live, target * cap + rank, -1)
    wide_slot = jnp.where(live, target * (cap + 1) + rank, -1)
    basis = basis_ref[...]

    def table_of(count, wanted):
        index = lax.broadcasted_iota(jnp.int32, (count, listed), 0)
        return jnp.where(index == wanted, 1.0, 0.0).astype(BF16)

    slot_table = table_of(slot_basis_ref.shape[0], slot)
    slot_basis = dot(slot_table, basis)
    slot_basis_ref[...] = slot_basis.astype(BF16)
    lift_basis_ref[...] = jnp.transpose(slot_basis).astype(BF16)
    wide_basis_ref[...] = dot(table_of(wide_basis_ref.shape[0], wide_slot), basis).astype(BF16)
    label = jnp.where(live, rows_ref[...] + 1, 0)
    lane = lax.broadcasted_iota(jnp.int32, labels_ref.shape, 1)
    index = lax.broadcasted_iota(jnp.int32, (labels_ref.shape[0], listed), 0)
    labels = jnp.zeros(labels_ref.shape, F32)
    for i in range(cap):
        wanted = jnp.where(rank == i, target * (cap + 1) + cap, -1)
        found = jnp.sum(jnp.where(index == wanted, label, 0), axis=1, keepdims=True)
        labels = jnp.where(lane == i, found.astype(F32), labels)
    labels_ref[...] = labels


def first_residual_kernel(peers_ref, loads_ref, incoming_ref, basis_ref, labels_ref, residual_ref, out_ref):
    mirrored(peers_ref, loads_ref, incoming_ref, residual_ref)
    out_ref[...] = product(basis_ref[...], 0.5 * residual_ref[...]) + labels_ref[...]


def residual_kernel(peers_ref, half_ref, incoming_ref, basis_ref, residual_ref, out_ref):
    mirrored(peers_ref, half_ref, incoming_ref, residual_ref)
    out_ref[...] = product(basis_ref[...], 0.5 * residual_ref[...])


def split_product(high, low, value):
    value_high, value_low = parts_of(value)
    return dot(
        jnp.concatenate([high, high, low], axis=1),
        jnp.concatenate([value_high, value_low, value_high], axis=0),
    )


def first_coarse_kernel(cap, stride, arrived_ref, block_ref, high_ref, low_ref, out_ref):
    slots, columns = out_ref.shape
    coarse_size = block_ref.shape[0]
    received = arrived_ref.shape[0]
    arrived = jnp.concatenate(parts_of(arrived_ref[...]), axis=1)
    slot = lax.broadcasted_iota(jnp.int32, (slots, received), 0)
    row = lax.broadcasted_iota(jnp.int32, (slots, received), 1)
    base = (slot // cap) * stride
    pick_value = (row == base + slot % cap).astype(F32).astype(BF16)
    pick_label = (row == base + cap).astype(F32).astype(BF16)
    values = dot(pick_value, arrived)
    values = values[:, :columns] + values[:, columns:]
    label_rows = dot(pick_label, arrived[:, :columns])
    lane = lax.broadcasted_iota(jnp.int32, (slots, columns), 1)
    own = lax.broadcasted_iota(jnp.int32, (slots, columns), 0) % cap
    labels = jnp.sum(jnp.where(lane == own, label_rows, 0.0), axis=1, keepdims=True)
    ids = lax.broadcasted_iota(jnp.int32, (slots, coarse_size), 1).astype(F32)
    owner = (labels - 1.0 == ids).astype(F32).astype(BF16)
    block_high, block_low = parts_of(block_ref[...])
    across = (((1,), (1,)), ((), ()))

    def composed(part):
        rows = dot(owner, part).astype(BF16)
        return lax.dot_general(rows, owner, across, preferred_element_type=F32).astype(BF16)

    high, low = composed(block_high), composed(block_low)
    high_ref[...] = high
    low_ref[...] = low
    out_ref[...] = split_product(high, low, values)


def coarse_kernel(high_ref, low_ref, values_ref, out_ref):
    out_ref[...] = split_product(high_ref[...], low_ref[...], values_ref[...])


def lift_kernel(
    peers_ref, inverse_ref, basis_ref, returned_ref, residual_ref, half_ref, out_ref, sum_ref
):
    residual = residual_ref[...]
    half = 0.25 * product(inverse_ref[...], residual) + product(basis_ref[...], returned_ref[...])
    half_ref[...] = half
    spread(peers_ref, half, out_ref)
    sum_ref[...] = column_sum(residual * half)


def operate_kernel(
    peers_ref, half_ref, incoming_ref, schur_ref, scale_ref, vector_ref, image_ref, out_ref, sum_ref
):
    mirrored(peers_ref, half_ref, incoming_ref, vector_ref)
    vector = vector_ref[...]
    image = scale_ref[...] * product(schur_ref[...], vector)
    image_ref[...] = image
    spread(peers_ref, image, out_ref)
    sum_ref[...] = column_sum(vector * image)


def last_kernel(
    peers_ref,
    half_ref,
    incoming_ref,
    schur_ref,
    scale_ref,
    energy_ref,
    first_ref,
    mixed_ref,
    vector_ref,
    out_ref,
):
    mirrored(peers_ref, half_ref, incoming_ref, vector_ref)
    vector = vector_ref[...]
    second = scale_ref[...] * column_sum(vector * product(schur_ref[...], vector))
    sums = jnp.concatenate([energy_ref[...], first_ref[...], mixed_ref[...], second], axis=0)
    out_ref[...] = jnp.broadcast_to(sums[None], out_ref.shape)


def regroup_kernel(sums_ref, out_ref):
    out_ref[...] = jnp.broadcast_to(jnp.sum(sums_ref[...], axis=0)[None], out_ref.shape)


def combine_kernel(sums_ref, first_ref, second_ref, out_ref):
    sums = jnp.sum(sums_ref[...], axis=0)
    energy, gram_first, gram_mixed, gram_second = (sums[i : i + 1] for i in range(4))
    step_first = energy / gram_first
    mixed_share = gram_mixed / gram_first
    step_second = (gram_mixed - gram_first / energy * gram_first) / (
        gram_second - mixed_share * gram_mixed
    )
    along_first = step_first + step_second * (step_first * mixed_share)
    along_second = step_second * step_first
    out_ref[...] = along_first * first_ref[...] - along_second * second_ref[...]


def call(kernel, scalars, inputs, outputs, flops=0, in_specs=None, scratch_shapes=()):
    moved = sum(x.size * x.dtype.itemsize for x in inputs)
    moved += sum(x.size * x.dtype.itemsize for x in outputs)
    single = len(outputs) == 1
    return pl.pallas_call(
        kernel,
        out_shape=outputs[0] if single else tuple(outputs),
        in_specs=in_specs or [SMEM] * len(scalars) + [VMEM] * len(inputs),
        out_specs=VMEM if single else tuple([VMEM] * len(outputs)),
        scratch_shapes=scratch_shapes,
        compiler_params=pltpu.CompilerParams(vmem_limit_bytes=20 << 20),
        cost_estimate=pl.CostEstimate(flops=flops, bytes_accessed=moved, transcendentals=0),
    )(*scalars, *inputs)


def body(
    loads,
    coefficient,
    schur_ref,
    schur_inverse,
    coarse_basis,
    partners,
    routes,
    coarse_rows,
    primal_count,
    coarse_inverse,
):
    rows_total, columns = loads.shape[2:]
    peers = partners[0, 0]
    tile_count = peers.shape[1]
    tile = rows_total // tile_count
    members = lax.axis_size("dom")
    groups = lax.axis_size("sub")
    primal_max = coarse_basis.shape[3]
    cap = max(2, (primal_max + groups - 1) // groups)
    stride = cap + 1
    slots = groups * cap
    load_tiles = loads[0, 0]
    inverse_local = schur_inverse[0, 0]

    def shaped(*shape, dtype=F32):
        return jax.ShapeDtypeStruct(shape, dtype)

    vector_shape = shaped(rows_total, columns)
    slot_shape = shaped(slots, columns)
    tiles_shape = shaped(members, tile, columns)
    sum_shape = shaped(1, columns)
    big = 4 * rows_total * rows_total * columns
    thin = 4 * rows_total * slots * columns

    plane = rotated(members, middle_of_plane(members))
    ring = rotated(groups, groups // 2)

    def exchange(tiles):
        return lax.all_to_all(tiles, "dom", 0, 0, tiled=True, axis_index_groups=[plane])

    def shift(values, per_group):
        grouped = values.reshape(groups, 1, per_group * columns)
        moved = lax.all_to_all(grouped, "sub", 0, 0, tiled=True, axis_index_groups=[ring])
        return moved.reshape(groups * per_group, columns)

    cores = 2
    chips = groups // cores
    layers = [
        [(z * cores + k) * members + d for k in range(cores) for d in plane]
        for z in rotated(chips, chips // 2)
    ]
    lines = [list(line) for line in zip(*layers)]

    def gather(values, sets):
        return lax.all_to_all(values, ("sub", "dom"), 0, 0, tiled=True, axis_index_groups=sets)

    given = [
        peers,
        routes.reshape(1, primal_max),
        coarse_rows[0],
        load_tiles,
        coarse_basis[0, 0].T,
    ]
    spaces = [pltpu.SMEM] + [pltpu.VMEM] * 4
    outgoing, slot_basis, wide_basis, lift_basis, labels, scale = call(
        functools.partial(first_kernel, cap),
        [primal_count, coefficient],
        [pltpu.with_memory_space_constraint(x, pltpu.HBM) for x in given],
        [
            tiles_shape,
            shaped(slots, rows_total, dtype=BF16),
            shaped(groups * stride, rows_total, dtype=BF16),
            shaped(rows_total, slots, dtype=BF16),
            shaped(groups * stride, columns),
            sum_shape,
        ],
        thin,
        in_specs=[SMEM] * 2 + [pl.BlockSpec(memory_space=pltpu.HBM)] * len(given),
        scratch_shapes=[space(x.shape, x.dtype) for space, x in zip(spaces, given)]
        + [pltpu.SemaphoreType.DMA((len(given),))],
    )
    incoming = exchange(outgoing)
    residual, outgoing = call(
        first_residual_kernel,
        [peers],
        [load_tiles, incoming, wide_basis, labels],
        [vector_shape, shaped(groups * stride, columns)],
        2 * thin,
    )
    arrived = shift(outgoing, stride)
    high, low, answer = call(
        functools.partial(first_coarse_kernel, cap, stride),
        [],
        [arrived, coarse_inverse[0, 0]],
        [shaped(slots, slots, dtype=BF16), shaped(slots, slots, dtype=BF16), slot_shape],
        20 * slots * slots * columns,
    )
    returned = shift(answer, cap)
    half, tiles, energy = call(
        lift_kernel,
        [peers],
        [inverse_local, lift_basis, returned, residual],
        [vector_shape, tiles_shape, sum_shape],
        big + thin,
    )
    incoming = exchange(tiles)
    first, half, tiles, gram_first = call(
        operate_kernel,
        [peers],
        [half, incoming, schur_ref, scale],
        [vector_shape, vector_shape, tiles_shape, sum_shape],
        big,
    )
    incoming = exchange(tiles)
    image, outgoing = call(
        residual_kernel, [peers], [half, incoming, slot_basis], [vector_shape, slot_shape], thin
    )
    arrived = shift(outgoing, cap)
    answer = call(coarse_kernel, [], [high, low, arrived], [slot_shape], 6 * slots * slots * columns)
    returned = shift(answer, cap)
    half, tiles, gram_mixed = call(
        lift_kernel,
        [peers],
        [inverse_local, lift_basis, returned, image],
        [vector_shape, tiles_shape, sum_shape],
        big + thin,
    )
    incoming = exchange(tiles)
    second, sums = call(
        last_kernel,
        [peers],
        [half, incoming, schur_ref, scale, energy, gram_first, gram_mixed],
        [vector_shape, shaped(cores * members, 4, columns)],
        big,
    )
    sums = call(regroup_kernel, [], [gather(sums, layers)], [shaped(chips, 4, columns)])
    sums = gather(sums, lines)
    solution = call(combine_kernel, [], [sums, first, second], [vector_shape])
    return solution.reshape(1, 1, rows_total, columns)


def solution(mesh):
    return jax.shard_map(
        body,
        mesh=mesh,
        in_specs=(
            P("sub", "dom", None, None),
            P("sub", "dom"),
            P(),
            P("sub", "dom", None, None),
            P("sub", "dom", None, None),
            P("sub", "dom", None, None),
            P("sub", "dom", None, None),
            P("sub", "dom", None),
            P("sub", "dom"),
            P("sub", "dom", None, None),
        ),
        out_specs=P("sub", "dom", None, None),
        check_vma=False,
    )
```

```python
import functools
import math

import jax
import jax.numpy as jnp
from jax import lax
from jax.experimental import pallas as pl
from jax.experimental.pallas import tpu as pltpu
from jax.sharding import PartitionSpec as P

F32 = jnp.float32
BF16 = jnp.bfloat16
VMEM = pl.BlockSpec(memory_space=pltpu.VMEM)
SMEM = pl.BlockSpec(memory_space=pltpu.SMEM)


def parts_of(value):
    high = value.astype(BF16)
    low = (value - high.astype(F32)).astype(BF16)
    return high, low


def dot(left, right):
    return jnp.dot(left, right, preferred_element_type=F32)


def product(matrix, value):
    columns = value.shape[1]
    both = dot(matrix, jnp.concatenate(parts_of(value), axis=1))
    return both[:, :columns] + both[:, columns:]


def row_product(value, matrix):
    rows = value.shape[0]
    both = dot(jnp.concatenate(parts_of(value), axis=0), matrix)
    return both[:rows] + both[rows:]


def middle_of_plane(members):
    side = math.isqrt(members)
    return side // 2 * side + side // 2


def rotated(count, first):
    return [(first + i) % count for i in range(count)]


def place_of(peers_ref, t, members):
    return lax.rem(peers_ref[0, t] + (members - middle_of_plane(members)), members)


def each_tile(blocks, tiles):
    return [(p, t) for p in range(blocks) for t in range(tiles)]


def block(ref, p, t, rows, lanes):
    return ref.at[p * rows : (p + 1) * rows, t * lanes : (t + 1) * lanes]


def first_kernel(
    cap,
    count_ref,
    stiffness_ref,
    peers_hbm,
    routes_hbm,
    rows_hbm,
    loads_hbm,
    basis_hbm,
    out_ref,
    slot_basis_ref,
    wide_basis_ref,
    labels_ref,
    peers_ref,
    listed_ref,
    routes_ref,
    rows_ref,
    loads_ref,
    basis_ref,
    about_ref,
    semaphores,
):
    sources = (peers_hbm, peers_hbm, routes_hbm, rows_hbm, loads_hbm, basis_hbm)
    targets = (peers_ref, listed_ref, routes_ref, rows_ref, loads_ref, basis_ref)
    copies = [
        pltpu.make_async_copy(source, target, semaphores.at[i])
        for i, (source, target) in enumerate(zip(sources, targets))
    ]
    for copy in copies:
        copy.start()
    about_ref[...] = jnp.full_like(about_ref, stiffness_ref[0, 0])
    for copy in copies:
        copy.wait()
    tile_count = listed_ref.shape[1]
    tile = loads_ref.shape[0] // tile_count
    members = out_ref.shape[0]
    about_ref[0:1, 0:tile_count] = listed_ref[0:1, :].astype(F32)
    out_ref[:, 0:tile] = jnp.zeros((members, tile, out_ref.shape[2]), F32)
    for m in range(members):
        out_ref[m, tile:] = about_ref[...]
    for t in range(tile_count):
        out_ref[place_of(peers_ref, t, members), 0:tile] = loads_ref[t * tile : (t + 1) * tile]
    groups = slot_basis_ref.shape[0] // cap
    target = lax.rem(routes_ref[...] + (groups - groups // 2), groups)
    listed = target.shape[1]
    first = lax.broadcasted_iota(jnp.int32, (listed, listed), 0)
    second = lax.broadcasted_iota(jnp.int32, (listed, listed), 1)
    column = jnp.sum(jnp.where(first == second, target, 0), axis=1, keepdims=True)
    ahead = jnp.where(first < second, 1, 0) * jnp.where(column == target, 1, 0)
    rank = jnp.sum(ahead, axis=0, keepdims=True)
    live = lax.broadcasted_iota(jnp.int32, target.shape, 1) < count_ref[0, 0]
    slot = jnp.where(live, target * cap + rank, -1)
    wide_slot = jnp.where(live, target * (cap + 1) + rank, -1)
    basis = basis_ref[...]

    def table_of(count, wanted):
        index = lax.broadcasted_iota(jnp.int32, (count, listed), 0)
        return jnp.where(index == wanted, 1.0, 0.0).astype(BF16)

    slot_table = table_of(slot_basis_ref.shape[0], slot)
    slot_basis_ref[...] = dot(slot_table, basis).astype(BF16)
    wide_basis_ref[...] = dot(table_of(wide_basis_ref.shape[0], wide_slot), basis).astype(BF16)
    label = jnp.where(live, rows_ref[...] + 1, 0)
    lane = lax.broadcasted_iota(jnp.int32, labels_ref.shape, 1)
    index = lax.broadcasted_iota(jnp.int32, (labels_ref.shape[0], listed), 0)
    labels = jnp.zeros(labels_ref.shape, F32)
    for i in range(cap):
        wanted = jnp.where(rank == i, target * (cap + 1) + cap, -1)
        found = jnp.sum(jnp.where(index == wanted, label, 0), axis=1, keepdims=True)
        labels = jnp.where(lane == i, found.astype(F32), labels)
    labels_ref[...] = labels


def first_residual_kernel(
    peers_ref,
    loads_ref,
    incoming_ref,
    basis_ref,
    labels_ref,
    residual_ref,
    out_ref,
    listed_ref,
    scale_ref,
    sum_ref,
):
    members = incoming_ref.shape[0]
    columns, rows_total = residual_ref.shape
    tile = rows_total // peers_ref.shape[1]
    share = columns // members
    for t in range(peers_ref.shape[1]):
        rows = slice(t * tile, (t + 1) * tile)
        total = loads_ref[rows] + incoming_ref[place_of(peers_ref, t, members), 0:tile]
        sum_ref[rows] = total
        residual_ref[:, rows] = jnp.transpose(total)
    out_ref[...] = product(basis_ref[...], 0.5 * sum_ref[...]) + labels_ref[...]
    turn = members - middle_of_plane(members)
    for m in range(members):
        listed = incoming_ref[m, tile : tile + 1].astype(jnp.int32)
        listed_ref[m : m + 1] = lax.rem(listed + turn, members)
        stiffness = incoming_ref[m, tile + 1 : tile + 2]
        scale_ref[m * share : (m + 1) * share] = jnp.broadcast_to(stiffness, (share, columns))


def residual_kernel(incoming_ref, basis_ref, residual_ref, out_ref):
    members, tiles, share, tile = incoming_ref.shape
    for p, t in each_tile(members, tiles):
        block(residual_ref, p, t, share, tile)[...] = incoming_ref[p, t]
    columns = residual_ref.shape[0]
    both = lax.dot_general(
        basis_ref[...],
        jnp.concatenate(parts_of(0.5 * residual_ref[...]), axis=0),
        (((1,), (1,)), ((), ())),
        preferred_element_type=F32,
    )
    out_ref[...] = both[:, :columns] + both[:, columns:]


def split_product(high, low, value):
    value_high, value_low = parts_of(value)
    return dot(
        jnp.concatenate([high, high, low], axis=1),
        jnp.concatenate([value_high, value_low, value_high], axis=0),
    )


def first_coarse_kernel(cap, stride, arrived_ref, block_ref, high_ref, low_ref, out_ref):
    slots, columns = out_ref.shape
    coarse_size = block_ref.shape[0]
    received = arrived_ref.shape[0]
    arrived = jnp.concatenate(parts_of(arrived_ref[...]), axis=1)
    slot = lax.broadcasted_iota(jnp.int32, (slots, received), 0)
    row = lax.broadcasted_iota(jnp.int32, (slots, received), 1)
    base = (slot // cap) * stride
    pick_value = (row == base + slot % cap).astype(F32).astype(BF16)
    pick_label = (row == base + cap).astype(F32).astype(BF16)
    values = dot(pick_value, arrived)
    values = values[:, :columns] + values[:, columns:]
    label_rows = dot(pick_label, arrived[:, :columns])
    lane = lax.broadcasted_iota(jnp.int32, (slots, columns), 1)
    own = lax.broadcasted_iota(jnp.int32, (slots, columns), 0) % cap
    labels = jnp.sum(jnp.where(lane == own, label_rows, 0.0), axis=1, keepdims=True)
    ids = lax.broadcasted_iota(jnp.int32, (slots, coarse_size), 1).astype(F32)
    owner = (labels - 1.0 == ids).astype(F32).astype(BF16)
    block_high, block_low = parts_of(block_ref[...])
    across = (((1,), (1,)), ((), ()))

    def composed(part):
        rows = dot(owner, part).astype(BF16)
        return lax.dot_general(rows, owner, across, preferred_element_type=F32).astype(BF16)

    high, low = composed(block_high), composed(block_low)
    high_ref[...] = high
    low_ref[...] = low
    out_ref[...] = split_product(high, low, values)


def coarse_kernel(high_ref, low_ref, values_ref, out_ref):
    out_ref[...] = split_product(high_ref[...], low_ref[...], values_ref[...])


def lift_kernel(inverse_ref, basis_ref, returned_ref, residual_ref, out_ref):
    members, tiles, share, tile = out_ref.shape
    rows_total = residual_ref.shape[1]
    residual = residual_ref[...]
    half = 0.25 * row_product(residual, inverse_ref[...])
    half = half + row_product(jnp.transpose(returned_ref[...]), basis_ref[...])
    for p, t in each_tile(members, rows_total // tile):
        out_ref[p, t] = half[p * share : (p + 1) * share, t * tile : (t + 1) * tile]
    if tiles > rows_total // tile:
        sums = jnp.sum(residual * half, axis=1, keepdims=True)
        for p in range(members):
            mine = sums[p * share : (p + 1) * share]
            out_ref[p, tiles - 1] = jnp.broadcast_to(mine, (share, tile))


def partner_places(listed_ref, place_ref, partner_ref, members, tiles):
    for e, t in each_tile(members, tiles):
        place_ref[listed_ref[e, t] * members + e] = t
    for p, t in each_tile(members, tiles):
        e = listed_ref[p, t]
        partner_ref[p * tiles + t] = e * tiles + place_ref[p * members + e]


def partner_of(partner_ref, p, t, tiles):
    flat = partner_ref[p * tiles + t]
    return lax.div(flat, tiles), lax.rem(flat, tiles)


def share_sums(value, share):
    rows = jnp.sum(value, axis=1, keepdims=True)
    return jnp.sum(rows.reshape(value.shape[0] // share, share, 1), axis=0)


def operate_kernel(
    listed_ref,
    incoming_ref,
    schur_ref,
    scale_ref,
    vector_ref,
    image_ref,
    out_ref,
    energy_ref,
    first_ref,
    partner_ref,
    place_ref,
    tiles_ref,
):
    members, tiles, share, tile = out_ref.shape
    partner_places(listed_ref, place_ref, partner_ref, members, tiles)
    for p, t in each_tile(members, tiles):
        other = incoming_ref[partner_of(partner_ref, p, t, tiles)]
        block(vector_ref, p, t, share, tile)[...] = incoming_ref[p, t] + other
    vector = vector_ref[...]
    image = scale_ref[:, 0:1] * row_product(vector, schur_ref[...])
    image_ref[...] = image
    for p, t in each_tile(members, tiles):
        tiles_ref[p, t] = image[p * share : (p + 1) * share, t * tile : (t + 1) * tile]
    for p, t in each_tile(members, tiles):
        out_ref[p, t] = tiles_ref[p, t] + tiles_ref[partner_of(partner_ref, p, t, tiles)]
    energy_ref[...] = jnp.sum(incoming_ref[:, tiles], axis=0)
    first_ref[...] = jnp.broadcast_to(share_sums(vector * image, share), first_ref.shape)


def entries_of(rows, columns, share, q):
    lane = lax.broadcasted_iota(jnp.int32, (rows, columns), 1)
    return lane == q * share + lax.broadcasted_iota(jnp.int32, (rows, columns), 0)


def last_kernel(
    partner_ref,
    incoming_ref,
    schur_ref,
    scale_ref,
    image_ref,
    energy_ref,
    first_ref,
    vector_ref,
    out_ref,
):
    members, tiles, share, tile = incoming_ref.shape
    for p, t in each_tile(members, tiles):
        other = incoming_ref[partner_of(partner_ref, p, t, tiles)]
        block(vector_ref, p, t, share, tile)[...] = incoming_ref[p, t] + other
    vector = vector_ref[...]
    product_rows = scale_ref[:, 0:1] * row_product(vector, schur_ref[...])
    sums = (
        energy_ref[:, 0:1],
        first_ref[:, 0:1],
        share_sums(vector * image_ref[...], share),
        share_sums(vector * product_rows, share),
    )
    columns = out_ref.shape[1]
    packed = jnp.zeros((share, columns), F32)
    for q, value in enumerate(sums):
        packed = jnp.where(entries_of(share, columns, share, q), value, packed)
    row = jnp.sum(packed, axis=0, keepdims=True)
    out_ref[...] = jnp.broadcast_to(row, out_ref.shape)


def combine_kernel(sums_ref, first_ref, second_ref, out_ref):
    members, tiles, share, tile = out_ref.shape
    columns = sums_ref.shape[1]
    row = jnp.sum(sums_ref[...], axis=0, keepdims=True)

    def total(q):
        mine = jnp.where(entries_of(share, columns, share, q), row, 0.0)
        return jnp.sum(mine, axis=1, keepdims=True)

    energy, gram_first, gram_mixed, gram_second = (total(q) for q in range(4))
    step_first = energy / gram_first
    mixed_share = gram_mixed / gram_first
    step_second = (gram_mixed - gram_first / energy * gram_first) / (
        gram_second - mixed_share * gram_mixed
    )
    along_first = step_first + step_second * (step_first * mixed_share)
    along_second = step_second * step_first
    for p, t in each_tile(members, tiles):
        here = block(first_ref, p, t, share, tile)[...]
        there = block(second_ref, p, t, share, tile)[...]
        out_ref[p, t] = along_first * here - along_second * there


def finish_kernel(incoming_ref, out_ref):
    members, tiles, share, tile = incoming_ref.shape
    for t in range(tiles):
        rows = incoming_ref[:, t].reshape(members * share, tile)
        out_ref[t * tile : (t + 1) * tile] = jnp.transpose(rows)


def call(kernel, scalars, inputs, outputs, flops=0, in_specs=None, out_specs=None, scratch_shapes=()):
    moved = sum(x.size * x.dtype.itemsize for x in inputs)
    moved += sum(x.size * x.dtype.itemsize for x in outputs)
    single = len(outputs) == 1
    specs = out_specs or [VMEM] * len(outputs)
    return pl.pallas_call(
        kernel,
        out_shape=outputs[0] if single else tuple(outputs),
        in_specs=in_specs or [SMEM] * len(scalars) + [VMEM] * len(inputs),
        out_specs=specs[0] if single else tuple(specs),
        scratch_shapes=scratch_shapes,
        compiler_params=pltpu.CompilerParams(vmem_limit_bytes=20 << 20),
        cost_estimate=pl.CostEstimate(flops=flops, bytes_accessed=moved, transcendentals=0),
    )(*scalars, *inputs)


def body(
    loads,
    coefficient,
    schur_ref,
    schur_inverse,
    coarse_basis,
    partners,
    routes,
    coarse_rows,
    primal_count,
    coarse_inverse,
):
    rows_total, columns = loads.shape[2:]
    peers = partners[0, 0]
    tile_count = peers.shape[1]
    tile = rows_total // tile_count
    members = lax.axis_size("dom")
    groups = lax.axis_size("sub")
    primal_max = coarse_basis.shape[3]
    cap = max(2, (primal_max + groups - 1) // groups)
    stride = cap + 1
    slots = groups * cap
    load_tiles = loads[0, 0]
    inverse_local = schur_inverse[0, 0]

    def shaped(*shape, dtype=F32):
        return jax.ShapeDtypeStruct(shape, dtype)

    share = columns // members
    vector_shape = shaped(columns, rows_total)
    slot_shape = shaped(slots, columns)
    tiles_shape = shaped(members, tile_count, share, tile)
    sum_shape = shaped(share, tile)
    big = 4 * rows_total * rows_total * columns
    thin = 4 * rows_total * slots * columns

    plane = rotated(members, middle_of_plane(members))
    ring = rotated(groups, groups // 2)

    def exchange(tiles):
        return lax.all_to_all(tiles, "dom", 0, 0, tiled=True, axis_index_groups=[plane])

    def shift(values, per_group):
        grouped = values.reshape(groups, 1, per_group * columns)
        moved = lax.all_to_all(grouped, "sub", 0, 0, tiled=True, axis_index_groups=[ring])
        return moved.reshape(groups * per_group, columns)

    given = [
        peers,
        routes.reshape(1, primal_max),
        coarse_rows[0],
        load_tiles,
        coarse_basis[0, 0].T,
    ]
    listed = [pltpu.SMEM(peers.shape, peers.dtype)]
    listed += [pltpu.VMEM(x.shape, x.dtype) for x in given]
    outgoing, slot_basis, wide_basis, labels = call(
        functools.partial(first_kernel, cap),
        [primal_count, coefficient],
        [pltpu.with_memory_space_constraint(x, pltpu.HBM) for x in given],
        [
            shaped(members, tile + 8, columns),
            shaped(slots, rows_total, dtype=BF16),
            shaped(groups * stride, rows_total, dtype=BF16),
            shaped(groups * stride, columns),
        ],
        thin,
        in_specs=[SMEM] * 2 + [pl.BlockSpec(memory_space=pltpu.HBM)] * len(given),
        scratch_shapes=listed
        + [pltpu.VMEM((8, columns), F32), pltpu.SemaphoreType.DMA((len(given) + 1,))],
    )
    residual, outgoing, listed, scale = call(
        first_residual_kernel,
        [peers],
        [load_tiles, exchange(outgoing), wide_basis, labels],
        [
            vector_shape,
            shaped(groups * stride, columns),
            shaped(members, columns, dtype=jnp.int32),
            shaped(columns, columns),
        ],
        2 * thin,
        scratch_shapes=[pltpu.VMEM((rows_total, columns), F32)],
    )
    arrived = shift(outgoing, stride)
    high, low, answer = call(
        functools.partial(first_coarse_kernel, cap, stride),
        [],
        [arrived, coarse_inverse[0, 0]],
        [shaped(slots, slots, dtype=BF16), shaped(slots, slots, dtype=BF16), slot_shape],
        20 * slots * slots * columns,
    )
    returned = shift(answer, cap)
    outgoing = call(
        lift_kernel,
        [],
        [inverse_local, slot_basis, returned, residual],
        [shaped(members, tile_count + 1, share, tile)],
        big + thin,
    )
    first, image, outgoing, energy, gram_first, partner = call(
        operate_kernel,
        [listed],
        [exchange(outgoing), schur_ref, scale],
        [
            vector_shape,
            vector_shape,
            tiles_shape,
            sum_shape,
            sum_shape,
            shaped(members * tile_count, dtype=jnp.int32),
        ],
        big,
        out_specs=[VMEM] * 5 + [SMEM],
        scratch_shapes=[
            pltpu.SMEM((members * members,), jnp.int32),
            pltpu.VMEM(tiles_shape.shape, F32),
        ],
    )
    residual, outgoing = call(
        residual_kernel, [], [exchange(outgoing), slot_basis], [vector_shape, slot_shape], thin
    )
    arrived = shift(outgoing, cap)
    answer = call(coarse_kernel, [], [high, low, arrived], [slot_shape], 6 * slots * slots * columns)
    returned = shift(answer, cap)
    outgoing = call(
        lift_kernel,
        [],
        [inverse_local, slot_basis, returned, residual],
        [tiles_shape],
        big + thin,
    )
    second, sums = call(
        last_kernel,
        [partner],
        [exchange(outgoing), schur_ref, scale, image, energy, gram_first],
        [vector_shape, shaped(groups, columns)],
        big,
    )
    outgoing = call(combine_kernel, [], [shift(sums, 1), first, second], [tiles_shape])
    solution = call(finish_kernel, [], [exchange(outgoing)], [shaped(rows_total, columns)])
    return solution.reshape(1, 1, rows_total, columns)


def solution(mesh):
    return jax.shard_map(
        body,
        mesh=mesh,
        in_specs=(
            P("sub", "dom", None, None),
            P("sub", "dom"),
            P(),
            P("sub", "dom", None, None),
            P("sub", "dom", None, None),
            P("sub", "dom", None, None),
            P("sub", "dom", None, None),
            P("sub", "dom", None),
            P("sub", "dom"),
            P("sub", "dom", None, None),
        ),
        out_specs=P("sub", "dom", None, None),
        check_vma=False,
    )
```

```python
import functools
import math

import jax
import jax.numpy as jnp
from jax import lax
from jax.experimental import pallas as pl
from jax.experimental.pallas import tpu as pltpu
from jax.sharding import PartitionSpec as P

F32 = jnp.float32
BF16 = jnp.bfloat16
VMEM = pl.BlockSpec(memory_space=pltpu.VMEM)
SMEM = pl.BlockSpec(memory_space=pltpu.SMEM)


def parts_of(value):
    high = value.astype(BF16)
    low = (value - high.astype(F32)).astype(BF16)
    return high, low


def dot(left, right):
    return jnp.dot(left, right, preferred_element_type=F32)


def product(matrix, value):
    columns = value.shape[1]
    both = dot(matrix, jnp.concatenate(parts_of(value), axis=1))
    return both[:, :columns] + both[:, columns:]


def row_product(value, matrix):
    rows = value.shape[0]
    both = dot(jnp.concatenate(parts_of(value), axis=0), matrix)
    return both[:rows] + both[rows:]


def middle_of_plane(members):
    side = math.isqrt(members)
    return side // 2 * side + side // 2


def rotated(count, first):
    return [(first + i) % count for i in range(count)]


def place_of(peers_ref, t, members):
    return lax.rem(peers_ref[0, t] + (members - middle_of_plane(members)), members)


def each_tile(blocks, tiles):
    return [(p, t) for p in range(blocks) for t in range(tiles)]


def block(ref, p, t, rows, lanes):
    return ref.at[p * rows : (p + 1) * rows, t * lanes : (t + 1) * lanes]


def first_kernel(
    cap,
    count_ref,
    stiffness_ref,
    peers_hbm,
    routes_hbm,
    rows_hbm,
    loads_hbm,
    basis_hbm,
    out_ref,
    slot_basis_ref,
    wide_basis_ref,
    labels_ref,
    peers_ref,
    listed_ref,
    routes_ref,
    rows_ref,
    loads_ref,
    basis_ref,
    about_ref,
    semaphores,
):
    sources = (peers_hbm, peers_hbm, routes_hbm, rows_hbm, basis_hbm, loads_hbm)
    targets = (peers_ref, listed_ref, routes_ref, rows_ref, basis_ref, loads_ref)
    copies = [
        pltpu.make_async_copy(source, target, semaphores.at[i])
        for i, (source, target) in enumerate(zip(sources, targets))
    ]
    for copy in copies:
        copy.start()
    about_ref[...] = jnp.full_like(about_ref, stiffness_ref[0, 0])
    tile_count = listed_ref.shape[1]
    tile = loads_ref.shape[0] // tile_count
    members = out_ref.shape[0]
    out_ref[:, 0:tile] = jnp.zeros((members, tile, out_ref.shape[2]), F32)
    for copy in copies[2:5]:
        copy.wait()
    groups = slot_basis_ref.shape[0] // cap
    target = lax.rem(routes_ref[...] + (groups - groups // 2), groups)
    listed = target.shape[1]
    first = lax.broadcasted_iota(jnp.int32, (listed, listed), 0)
    second = lax.broadcasted_iota(jnp.int32, (listed, listed), 1)
    column = jnp.sum(jnp.where(first == second, target, 0), axis=1, keepdims=True)
    ahead = jnp.where(first < second, 1, 0) * jnp.where(column == target, 1, 0)
    rank = jnp.sum(ahead, axis=0, keepdims=True)
    live = lax.broadcasted_iota(jnp.int32, target.shape, 1) < count_ref[0, 0]
    slot = jnp.where(live, target * cap + rank, -1)
    wide_slot = jnp.where(live, target * (cap + 1) + rank, -1)
    basis = basis_ref[...]

    def table_of(count, wanted):
        index = lax.broadcasted_iota(jnp.int32, (count, listed), 0)
        return jnp.where(index == wanted, 1.0, 0.0).astype(BF16)

    slot_table = table_of(slot_basis_ref.shape[0], slot)
    slot_basis_ref[...] = dot(slot_table, basis).astype(BF16)
    wide_basis_ref[...] = dot(table_of(wide_basis_ref.shape[0], wide_slot), basis).astype(BF16)
    label = jnp.where(live, rows_ref[...] + 1, 0)
    lane = lax.broadcasted_iota(jnp.int32, labels_ref.shape, 1)
    index = lax.broadcasted_iota(jnp.int32, (labels_ref.shape[0], listed), 0)
    labels = jnp.zeros(labels_ref.shape, F32)
    for i in range(cap):
        wanted = jnp.where(rank == i, target * (cap + 1) + cap, -1)
        found = jnp.sum(jnp.where(index == wanted, label, 0), axis=1, keepdims=True)
        labels = jnp.where(lane == i, found.astype(F32), labels)
    labels_ref[...] = labels
    for copy in copies[:2] + copies[5:]:
        copy.wait()
    about_ref[0:1, 0:tile_count] = listed_ref[0:1, :].astype(F32)
    for m in range(members):
        out_ref[m, tile:] = about_ref[...]
    for t in range(tile_count):
        out_ref[place_of(peers_ref, t, members), 0:tile] = loads_ref[t * tile : (t + 1) * tile]


def first_residual_kernel(
    peers_ref,
    loads_ref,
    incoming_ref,
    basis_ref,
    labels_ref,
    residual_ref,
    out_ref,
    partner_ref,
    scale_ref,
    sum_ref,
    listed_ref,
):
    members = incoming_ref.shape[0]
    columns, rows_total = residual_ref.shape
    tile = rows_total // peers_ref.shape[1]
    share = columns // members
    for t in range(peers_ref.shape[1]):
        rows = slice(t * tile, (t + 1) * tile)
        total = loads_ref[rows] + incoming_ref[place_of(peers_ref, t, members), 0:tile]
        sum_ref[rows] = total
        residual_ref[:, rows] = jnp.transpose(total)
    out_ref[...] = product(basis_ref[...], 0.5 * sum_ref[...]) + labels_ref[...]
    turn = members - middle_of_plane(members)
    for m in range(members):
        listed = incoming_ref[m, tile : tile + 1].astype(jnp.int32)
        listed_ref[m : m + 1] = lax.rem(listed + turn, members)
        stiffness = incoming_ref[m, tile + 1 : tile + 2]
        scale_ref[m * share : (m + 1) * share] = jnp.broadcast_to(stiffness, (share, columns))
    partner_ref[...] = partner_places(listed_ref[...], peers_ref.shape[1])


def residual_kernel(incoming_ref, basis_ref, residual_ref, out_ref):
    members, tiles, share, tile = incoming_ref.shape
    for p, t in each_tile(members, tiles):
        block(residual_ref, p, t, share, tile)[...] = incoming_ref[p, t]
    columns = residual_ref.shape[0]
    both = lax.dot_general(
        basis_ref[...],
        jnp.concatenate(parts_of(0.5 * residual_ref[...]), axis=0),
        (((1,), (1,)), ((), ())),
        preferred_element_type=F32,
    )
    out_ref[...] = both[:, :columns] + both[:, columns:]


def split_product(high, low, value):
    value_high, value_low = parts_of(value)
    return dot(
        jnp.concatenate([high, high, low], axis=1),
        jnp.concatenate([value_high, value_low, value_high], axis=0),
    )


def first_coarse_kernel(cap, stride, arrived_ref, block_ref, high_ref, low_ref, out_ref):
    slots, columns = out_ref.shape
    coarse_size = block_ref.shape[0]
    received = arrived_ref.shape[0]
    arrived = jnp.concatenate(parts_of(arrived_ref[...]), axis=1)
    slot = lax.broadcasted_iota(jnp.int32, (slots, received), 0)
    row = lax.broadcasted_iota(jnp.int32, (slots, received), 1)
    base = (slot // cap) * stride
    pick_value = (row == base + slot % cap).astype(F32).astype(BF16)
    pick_label = (row == base + cap).astype(F32).astype(BF16)
    values = dot(pick_value, arrived)
    values = values[:, :columns] + values[:, columns:]
    label_rows = dot(pick_label, arrived[:, :columns])
    lane = lax.broadcasted_iota(jnp.int32, (slots, columns), 1)
    own = lax.broadcasted_iota(jnp.int32, (slots, columns), 0) % cap
    labels = jnp.sum(jnp.where(lane == own, label_rows, 0.0), axis=1, keepdims=True)
    ids = lax.broadcasted_iota(jnp.int32, (slots, coarse_size), 1).astype(F32)
    owner = (labels - 1.0 == ids).astype(F32).astype(BF16)
    block_high, block_low = parts_of(block_ref[...])
    across = (((1,), (1,)), ((), ()))

    def composed(part):
        rows = dot(owner, part).astype(BF16)
        return lax.dot_general(rows, owner, across, preferred_element_type=F32).astype(BF16)

    high, low = composed(block_high), composed(block_low)
    high_ref[...] = high
    low_ref[...] = low
    out_ref[...] = split_product(high, low, values)


def coarse_kernel(high_ref, low_ref, values_ref, out_ref):
    out_ref[...] = split_product(high_ref[...], low_ref[...], values_ref[...])


def lift_kernel(inverse_ref, basis_ref, returned_ref, residual_ref, out_ref):
    members, tiles, share, tile = out_ref.shape
    rows_total = residual_ref.shape[1]
    half = 0.25 * row_product(residual_ref[...], inverse_ref[...])
    half = half + row_product(jnp.transpose(returned_ref[...]), basis_ref[...])
    for p, t in each_tile(members, rows_total // tile):
        out_ref[p, t] = half[p * share : (p + 1) * share, t * tile : (t + 1) * tile]
    if tiles > rows_total // tile:
        sums = jnp.sum(residual_ref[...] * half, axis=1, keepdims=True)
        for p in range(members):
            mine = sums[p * share : (p + 1) * share]
            out_ref[p, tiles - 1] = jnp.broadcast_to(mine, (share, tile))


def partner_places(listed, tiles):
    members = listed.shape[0]
    lane = lax.broadcasted_iota(jnp.int32, listed.shape, 1)
    member = lax.broadcasted_iota(jnp.int32, listed.shape, 0)
    empty = jnp.zeros((listed.shape[1] - members, listed.shape[1]), F32)
    across = jnp.transpose(jnp.concatenate([listed.astype(F32), empty], axis=0)).astype(jnp.int32)
    found = jnp.zeros(listed.shape, jnp.int32)
    for t in range(tiles):
        found = jnp.where(across[t : t + 1] == member, t, found)
    places = listed
    for t in range(tiles):
        mine = jnp.where(lane == listed[:, t : t + 1], found, 0)
        place = jnp.sum(mine, axis=1, keepdims=True)
        places = jnp.where(lane == tiles + t, place, places)
    return places


def partner_of(partner_ref, p, t, tiles):
    return partner_ref[p, t], partner_ref[p, tiles + t]


def share_sums(value, share):
    rows = jnp.sum(value, axis=1, keepdims=True)
    return jnp.sum(rows.reshape(value.shape[0] // share, share, 1), axis=0)


def operate_kernel(
    partner_ref,
    incoming_ref,
    schur_ref,
    scale_ref,
    vector_ref,
    image_ref,
    out_ref,
    energy_ref,
    first_ref,
    tiles_ref,
):
    members, tiles, share, tile = out_ref.shape
    for p, t in each_tile(members, tiles):
        other = incoming_ref[partner_of(partner_ref, p, t, tiles)]
        block(vector_ref, p, t, share, tile)[...] = incoming_ref[p, t] + other
    vector = vector_ref[...]
    image = scale_ref[:, 0:1] * row_product(vector, schur_ref[...])
    image_ref[...] = image
    for p, t in each_tile(members, tiles):
        tiles_ref[p, t] = image[p * share : (p + 1) * share, t * tile : (t + 1) * tile]
    for p, t in each_tile(members, tiles):
        out_ref[p, t] = tiles_ref[p, t] + tiles_ref[partner_of(partner_ref, p, t, tiles)]
    energy_ref[...] = jnp.sum(incoming_ref[:, tiles], axis=0)
    first_ref[...] = jnp.broadcast_to(share_sums(vector * image, share), first_ref.shape)


def entries_of(rows, columns, share, q):
    lane = lax.broadcasted_iota(jnp.int32, (rows, columns), 1)
    return lane == q * share + lax.broadcasted_iota(jnp.int32, (rows, columns), 0)


def last_kernel(
    partner_ref,
    incoming_ref,
    schur_ref,
    scale_ref,
    image_ref,
    energy_ref,
    first_ref,
    vector_ref,
    out_ref,
):
    members, tiles, share, tile = incoming_ref.shape
    for p, t in each_tile(members, tiles):
        other = incoming_ref[partner_of(partner_ref, p, t, tiles)]
        block(vector_ref, p, t, share, tile)[...] = incoming_ref[p, t] + other
    vector = vector_ref[...]
    product_rows = scale_ref[:, 0:1] * row_product(vector, schur_ref[...])
    sums = (
        energy_ref[:, 0:1],
        first_ref[:, 0:1],
        share_sums(vector * image_ref[...], share),
        share_sums(vector * product_rows, share),
    )
    columns = out_ref.shape[1]
    packed = jnp.zeros((share, columns), F32)
    for q, value in enumerate(sums):
        packed = jnp.where(entries_of(share, columns, share, q), value, packed)
    row = jnp.sum(packed, axis=0, keepdims=True)
    out_ref[...] = jnp.broadcast_to(row, out_ref.shape)


def combine_kernel(sums_ref, first_ref, second_ref, out_ref):
    members, tiles, share, tile = out_ref.shape
    columns = sums_ref.shape[1]
    row = jnp.sum(sums_ref[...], axis=0, keepdims=True)

    def total(q):
        mine = jnp.where(entries_of(share, columns, share, q), row, 0.0)
        return jnp.sum(mine, axis=1, keepdims=True)

    energy, gram_first, gram_mixed, gram_second = (total(q) for q in range(4))
    step_first = energy / gram_first
    mixed_share = gram_mixed / gram_first
    step_second = (gram_mixed - gram_first / energy * gram_first) / (
        gram_second - mixed_share * gram_mixed
    )
    along_first = step_first + step_second * (step_first * mixed_share)
    along_second = step_second * step_first
    for p, t in each_tile(members, tiles):
        here = block(first_ref, p, t, share, tile)[...]
        there = block(second_ref, p, t, share, tile)[...]
        out_ref[p, t] = along_first * here - along_second * there


def finish_kernel(incoming_ref, out_ref):
    members, tiles, share, tile = incoming_ref.shape
    for t in range(tiles):
        rows = incoming_ref[:, t].reshape(members * share, tile)
        out_ref[t * tile : (t + 1) * tile] = jnp.transpose(rows)


def call(kernel, scalars, inputs, outputs, flops=0, in_specs=None, out_specs=None, scratch_shapes=()):
    moved = sum(x.size * x.dtype.itemsize for x in inputs)
    moved += sum(x.size * x.dtype.itemsize for x in outputs)
    single = len(outputs) == 1
    specs = out_specs or [VMEM] * len(outputs)
    return pl.pallas_call(
        kernel,
        out_shape=outputs[0] if single else tuple(outputs),
        in_specs=in_specs or [SMEM] * len(scalars) + [VMEM] * len(inputs),
        out_specs=specs[0] if single else tuple(specs),
        scratch_shapes=scratch_shapes,
        compiler_params=pltpu.CompilerParams(vmem_limit_bytes=20 << 20),
        cost_estimate=pl.CostEstimate(flops=flops, bytes_accessed=moved, transcendentals=0),
    )(*scalars, *inputs)


def body(
    loads,
    coefficient,
    schur_ref,
    schur_inverse,
    coarse_basis,
    partners,
    routes,
    coarse_rows,
    primal_count,
    coarse_inverse,
):
    rows_total, columns = loads.shape[2:]
    peers = partners[0, 0]
    tile_count = peers.shape[1]
    tile = rows_total // tile_count
    members = lax.axis_size("dom")
    groups = lax.axis_size("sub")
    primal_max = coarse_basis.shape[3]
    cap = max(2, (primal_max + groups - 1) // groups)
    stride = cap + 1
    slots = groups * cap
    load_tiles = loads[0, 0]
    inverse_local = schur_inverse[0, 0]

    def shaped(*shape, dtype=F32):
        return jax.ShapeDtypeStruct(shape, dtype)

    share = columns // members
    vector_shape = shaped(columns, rows_total)
    slot_shape = shaped(slots, columns)
    tiles_shape = shaped(members, tile_count, share, tile)
    sum_shape = shaped(share, tile)
    big = 4 * rows_total * rows_total * columns
    thin = 4 * rows_total * slots * columns

    plane = rotated(members, middle_of_plane(members))
    ring = rotated(groups, groups // 2)

    def exchange(tiles):
        return lax.all_to_all(tiles, "dom", 0, 0, tiled=True, axis_index_groups=[plane])

    def shift(values, per_group):
        grouped = values.reshape(groups, 1, per_group * columns)
        moved = lax.all_to_all(grouped, "sub", 0, 0, tiled=True, axis_index_groups=[ring])
        return moved.reshape(groups * per_group, columns)

    given = [
        peers,
        routes.reshape(1, primal_max),
        coarse_rows[0],
        load_tiles,
        coarse_basis[0, 0].T,
    ]
    listed = [pltpu.SMEM(peers.shape, peers.dtype)]
    listed += [pltpu.VMEM(x.shape, x.dtype) for x in given]
    outgoing, slot_basis, wide_basis, labels = call(
        functools.partial(first_kernel, cap),
        [primal_count, coefficient],
        [pltpu.with_memory_space_constraint(x, pltpu.HBM) for x in given],
        [
            shaped(members, tile + 8, columns),
            shaped(slots, rows_total, dtype=BF16),
            shaped(groups * stride, rows_total, dtype=BF16),
            shaped(groups * stride, columns),
        ],
        thin,
        in_specs=[SMEM] * 2 + [pl.BlockSpec(memory_space=pltpu.HBM)] * len(given),
        scratch_shapes=listed
        + [pltpu.VMEM((8, columns), F32), pltpu.SemaphoreType.DMA((len(given) + 1,))],
    )
    residual, outgoing, partner, scale = call(
        first_residual_kernel,
        [peers],
        [load_tiles, exchange(outgoing), wide_basis, labels],
        [
            vector_shape,
            shaped(groups * stride, columns),
            shaped(members, columns, dtype=jnp.int32),
            shaped(columns, columns),
        ],
        2 * thin,
        scratch_shapes=[
            pltpu.VMEM((rows_total, columns), F32),
            pltpu.VMEM((members, columns), jnp.int32),
        ],
    )
    arrived = shift(outgoing, stride)
    high, low, answer = call(
        functools.partial(first_coarse_kernel, cap, stride),
        [],
        [arrived, coarse_inverse[0, 0]],
        [shaped(slots, slots, dtype=BF16), shaped(slots, slots, dtype=BF16), slot_shape],
        20 * slots * slots * columns,
    )
    returned = shift(answer, cap)
    outgoing = call(
        lift_kernel,
        [],
        [inverse_local, slot_basis, returned, residual],
        [shaped(members, tile_count + 1, share, tile)],
        big + thin,
    )
    first, image, outgoing, energy, gram_first = call(
        operate_kernel,
        [partner],
        [exchange(outgoing), schur_ref, scale],
        [
            vector_shape,
            vector_shape,
            tiles_shape,
            sum_shape,
            sum_shape,
        ],
        big,
        scratch_shapes=[pltpu.VMEM(tiles_shape.shape, F32)],
    )
    residual, outgoing = call(
        residual_kernel, [], [exchange(outgoing), slot_basis], [vector_shape, slot_shape], thin
    )
    arrived = shift(outgoing, cap)
    answer = call(coarse_kernel, [], [high, low, arrived], [slot_shape], 6 * slots * slots * columns)
    returned = shift(answer, cap)
    outgoing = call(
        lift_kernel,
        [],
        [inverse_local, slot_basis, returned, residual],
        [tiles_shape],
        big + thin,
    )
    second, sums = call(
        last_kernel,
        [partner],
        [exchange(outgoing), schur_ref, scale, image, energy, gram_first],
        [vector_shape, shaped(groups, columns)],
        big,
    )
    outgoing = call(combine_kernel, [], [shift(sums, 1), first, second], [tiles_shape])
    solution = call(finish_kernel, [], [exchange(outgoing)], [shaped(rows_total, columns)])
    return solution.reshape(1, 1, rows_total, columns)


def solution(mesh):
    return jax.shard_map(
        body,
        mesh=mesh,
        in_specs=(
            P("sub", "dom", None, None),
            P("sub", "dom"),
            P(),
            P("sub", "dom", None, None),
            P("sub", "dom", None, None),
            P("sub", "dom", None, None),
            P("sub", "dom", None, None),
            P("sub", "dom", None),
            P("sub", "dom"),
            P("sub", "dom", None, None),
        ),
        out_specs=P("sub", "dom", None, None),
        check_vma=False,
    )
```

```python
import functools
import math

import jax
import jax.numpy as jnp
from jax import lax
from jax.experimental import pallas as pl
from jax.experimental.pallas import tpu as pltpu
from jax.sharding import PartitionSpec as P

F32 = jnp.float32
BF16 = jnp.bfloat16
VMEM = pl.BlockSpec(memory_space=pltpu.VMEM)
SMEM = pl.BlockSpec(memory_space=pltpu.SMEM)


def parts_of(value):
    high = value.astype(BF16)
    low = (value - high.astype(F32)).astype(BF16)
    return high, low


def dot(left, right):
    return jnp.dot(left, right, preferred_element_type=F32)


def product(matrix, value):
    columns = value.shape[1]
    both = dot(matrix, jnp.concatenate(parts_of(value), axis=1))
    return both[:, :columns] + both[:, columns:]


def row_product(value, matrix):
    rows = value.shape[0]
    both = dot(jnp.concatenate(parts_of(value), axis=0), matrix)
    return both[:rows] + both[rows:]


def middle_of_plane(members):
    side = math.isqrt(members)
    return side // 2 * side + side // 2


def rotated(count, first):
    return [(first + i) % count for i in range(count)]


def place_of(peers_ref, t, members):
    return lax.rem(peers_ref[0, t] + (members - middle_of_plane(members)), members)


def each_tile(blocks, tiles):
    return [(p, t) for p in range(blocks) for t in range(tiles)]


def block(ref, p, t, rows, lanes):
    return ref.at[p * rows : (p + 1) * rows, t * lanes : (t + 1) * lanes]


def first_kernel(
    cap,
    count_ref,
    stiffness_ref,
    peers_hbm,
    routes_hbm,
    rows_hbm,
    loads_hbm,
    basis_hbm,
    out_ref,
    slot_basis_ref,
    wide_basis_ref,
    labels_ref,
    peers_ref,
    listed_ref,
    routes_ref,
    rows_ref,
    loads_ref,
    basis_ref,
    about_ref,
    semaphores,
):
    sources = (peers_hbm, peers_hbm, routes_hbm, rows_hbm, basis_hbm, loads_hbm)
    targets = (peers_ref, listed_ref, routes_ref, rows_ref, basis_ref, loads_ref)
    copies = [
        pltpu.make_async_copy(source, target, semaphores.at[i])
        for i, (source, target) in enumerate(zip(sources, targets))
    ]
    for copy in copies:
        copy.start()
    about_ref[...] = jnp.full_like(about_ref, stiffness_ref[0, 0])
    tile_count = listed_ref.shape[1]
    tile = loads_ref.shape[0] // tile_count
    members = out_ref.shape[0]
    out_ref[:, 0:tile] = jnp.zeros((members, tile, out_ref.shape[2]), F32)
    for copy in copies[2:5]:
        copy.wait()
    groups = slot_basis_ref.shape[0] // cap
    target = lax.rem(routes_ref[...] + (groups - groups // 2), groups)
    listed = target.shape[1]
    first = lax.broadcasted_iota(jnp.int32, (listed, listed), 0)
    second = lax.broadcasted_iota(jnp.int32, (listed, listed), 1)
    column = jnp.sum(jnp.where(first == second, target, 0), axis=1, keepdims=True)
    ahead = jnp.where(first < second, 1, 0) * jnp.where(column == target, 1, 0)
    rank = jnp.sum(ahead, axis=0, keepdims=True)
    live = lax.broadcasted_iota(jnp.int32, target.shape, 1) < count_ref[0, 0]
    slot = jnp.where(live, target * cap + rank, -1)
    wide_slot = jnp.where(live, target * (cap + 1) + rank, -1)
    basis = basis_ref[...]

    def table_of(count, wanted):
        index = lax.broadcasted_iota(jnp.int32, (count, listed), 0)
        return jnp.where(index == wanted, 1.0, 0.0).astype(BF16)

    slot_table = table_of(slot_basis_ref.shape[0], slot)
    slot_basis_ref[...] = dot(slot_table, basis).astype(BF16)
    wide_basis_ref[...] = dot(table_of(wide_basis_ref.shape[0], wide_slot), basis).astype(BF16)
    label = jnp.where(live, rows_ref[...] + 1, 0)
    lane = lax.broadcasted_iota(jnp.int32, labels_ref.shape, 1)
    index = lax.broadcasted_iota(jnp.int32, (labels_ref.shape[0], listed), 0)
    labels = jnp.zeros(labels_ref.shape, F32)
    for i in range(cap):
        wanted = jnp.where(rank == i, target * (cap + 1) + cap, -1)
        found = jnp.sum(jnp.where(index == wanted, label, 0), axis=1, keepdims=True)
        labels = jnp.where(lane == i, found.astype(F32), labels)
    labels_ref[...] = labels
    for copy in copies[:2] + copies[5:]:
        copy.wait()
    about_ref[0:1, 0:tile_count] = listed_ref[0:1, :].astype(F32)
    for m in range(members):
        out_ref[m, tile:] = about_ref[...]
    for t in range(tile_count):
        out_ref[place_of(peers_ref, t, members), 0:tile] = loads_ref[t * tile : (t + 1) * tile]


def first_residual_kernel(
    peers_ref,
    loads_ref,
    incoming_ref,
    basis_ref,
    labels_ref,
    residual_ref,
    out_ref,
    listed_ref,
    scale_ref,
    sum_ref,
):
    members = incoming_ref.shape[0]
    columns, rows_total = residual_ref.shape
    tile = rows_total // peers_ref.shape[1]
    share = columns // members
    for t in range(peers_ref.shape[1]):
        rows = slice(t * tile, (t + 1) * tile)
        total = loads_ref[rows] + incoming_ref[place_of(peers_ref, t, members), 0:tile]
        sum_ref[rows] = total
        residual_ref[:, rows] = jnp.transpose(total)
    out_ref[...] = product(basis_ref[...], 0.5 * sum_ref[...]) + labels_ref[...]
    turn = members - middle_of_plane(members)
    for m in range(members):
        listed = incoming_ref[m, tile : tile + 1].astype(jnp.int32)
        listed_ref[m : m + 1] = lax.rem(listed + turn, members)
        stiffness = incoming_ref[m, tile + 1 : tile + 2]
        scale_ref[m * share : (m + 1) * share] = jnp.broadcast_to(stiffness, (share, columns))


def residual_kernel(incoming_ref, basis_ref, residual_ref, out_ref):
    members, tiles, share, tile = incoming_ref.shape
    for p, t in each_tile(members, tiles):
        block(residual_ref, p, t, share, tile)[...] = incoming_ref[p, t]
    columns = residual_ref.shape[0]
    both = lax.dot_general(
        basis_ref[...],
        jnp.concatenate(parts_of(0.5 * residual_ref[...]), axis=0),
        (((1,), (1,)), ((), ())),
        preferred_element_type=F32,
    )
    out_ref[...] = both[:, :columns] + both[:, columns:]


def split_product(high, low, value):
    value_high, value_low = parts_of(value)
    return dot(
        jnp.concatenate([high, high, low], axis=1),
        jnp.concatenate([value_high, value_low, value_high], axis=0),
    )


def first_coarse_kernel(cap, stride, arrived_ref, block_ref, high_ref, low_ref, out_ref):
    slots, columns = out_ref.shape
    coarse_size = block_ref.shape[0]
    received = arrived_ref.shape[0]
    arrived = jnp.concatenate(parts_of(arrived_ref[...]), axis=1)
    slot = lax.broadcasted_iota(jnp.int32, (slots, received), 0)
    row = lax.broadcasted_iota(jnp.int32, (slots, received), 1)
    base = (slot // cap) * stride
    pick_value = (row == base + slot % cap).astype(F32).astype(BF16)
    pick_label = (row == base + cap).astype(F32).astype(BF16)
    values = dot(pick_value, arrived)
    values = values[:, :columns] + values[:, columns:]
    label_rows = dot(pick_label, arrived[:, :columns])
    lane = lax.broadcasted_iota(jnp.int32, (slots, columns), 1)
    own = lax.broadcasted_iota(jnp.int32, (slots, columns), 0) % cap
    labels = jnp.sum(jnp.where(lane == own, label_rows, 0.0), axis=1, keepdims=True)
    ids = lax.broadcasted_iota(jnp.int32, (slots, coarse_size), 1).astype(F32)
    owner = (labels - 1.0 == ids).astype(F32).astype(BF16)
    block_high, block_low = parts_of(block_ref[...])
    across = (((1,), (1,)), ((), ()))

    def composed(part):
        rows = dot(owner, part).astype(BF16)
        return lax.dot_general(rows, owner, across, preferred_element_type=F32).astype(BF16)

    high, low = composed(block_high), composed(block_low)
    high_ref[...] = high
    low_ref[...] = low
    out_ref[...] = split_product(high, low, values)


def coarse_kernel(high_ref, low_ref, values_ref, out_ref):
    out_ref[...] = split_product(high_ref[...], low_ref[...], values_ref[...])


def lift_kernel(inverse_ref, basis_ref, returned_ref, residual_ref, out_ref):
    members, tiles, share, tile = out_ref.shape
    rows_total = residual_ref.shape[1]
    half = 0.25 * row_product(residual_ref[...], inverse_ref[...])
    half = half + row_product(jnp.transpose(returned_ref[...]), basis_ref[...])
    for p, t in each_tile(members, rows_total // tile):
        out_ref[p, t] = half[p * share : (p + 1) * share, t * tile : (t + 1) * tile]
    if tiles > rows_total // tile:
        sums = jnp.sum(residual_ref[...] * half, axis=1, keepdims=True)
        for p in range(members):
            mine = sums[p * share : (p + 1) * share]
            out_ref[p, tiles - 1] = jnp.broadcast_to(mine, (share, tile))


def partner_places(listed, tiles):
    members = listed.shape[0]
    lane = lax.broadcasted_iota(jnp.int32, listed.shape, 1)
    member = lax.broadcasted_iota(jnp.int32, listed.shape, 0)
    empty = jnp.zeros((listed.shape[1] - members, listed.shape[1]), F32)
    across = jnp.transpose(jnp.concatenate([listed.astype(F32), empty], axis=0)).astype(jnp.int32)
    found = jnp.zeros(listed.shape, jnp.int32)
    for t in range(tiles):
        found = jnp.where(across[t : t + 1] == member, t, found)
    places = listed
    for t in range(tiles):
        mine = jnp.where(lane == listed[:, t : t + 1], found, 0)
        place = jnp.sum(mine, axis=1, keepdims=True)
        places = jnp.where(lane == tiles + t, place, places)
    return places


def first_lift_kernel(
    inverse_ref, basis_ref, returned_ref, residual_ref, listed_ref, out_ref, partner_ref
):
    partner_ref[...] = partner_places(listed_ref[...], out_ref.shape[1] - 1)
    lift_kernel(inverse_ref, basis_ref, returned_ref, residual_ref, out_ref)


def partner_of(partner_ref, p, t, tiles):
    return partner_ref[p, t], partner_ref[p, tiles + t]


def share_sums(value, share):
    rows = jnp.sum(value, axis=1, keepdims=True)
    return jnp.sum(rows.reshape(value.shape[0] // share, share, 1), axis=0)


def operate_kernel(
    partner_ref,
    incoming_ref,
    schur_ref,
    scale_ref,
    vector_ref,
    image_ref,
    out_ref,
    energy_ref,
    first_ref,
    tiles_ref,
):
    members, tiles, share, tile = out_ref.shape
    for p, t in each_tile(members, tiles):
        other = incoming_ref[partner_of(partner_ref, p, t, tiles)]
        block(vector_ref, p, t, share, tile)[...] = incoming_ref[p, t] + other
    vector = vector_ref[...]
    image = scale_ref[:, 0:1] * row_product(vector, schur_ref[...])
    image_ref[...] = image
    for p, t in each_tile(members, tiles):
        tiles_ref[p, t] = image[p * share : (p + 1) * share, t * tile : (t + 1) * tile]
    for p, t in each_tile(members, tiles):
        out_ref[p, t] = tiles_ref[p, t] + tiles_ref[partner_of(partner_ref, p, t, tiles)]
    energy_ref[...] = jnp.sum(incoming_ref[:, tiles], axis=0)
    first_ref[...] = jnp.broadcast_to(share_sums(vector * image, share), first_ref.shape)


def entries_of(rows, columns, share, q):
    lane = lax.broadcasted_iota(jnp.int32, (rows, columns), 1)
    return lane == q * share + lax.broadcasted_iota(jnp.int32, (rows, columns), 0)


def last_kernel(
    partner_ref,
    incoming_ref,
    schur_ref,
    scale_ref,
    image_ref,
    energy_ref,
    first_ref,
    vector_ref,
    out_ref,
):
    members, tiles, share, tile = incoming_ref.shape
    for p, t in each_tile(members, tiles):
        other = incoming_ref[partner_of(partner_ref, p, t, tiles)]
        block(vector_ref, p, t, share, tile)[...] = incoming_ref[p, t] + other
    vector = vector_ref[...]
    product_rows = scale_ref[:, 0:1] * row_product(vector, schur_ref[...])
    sums = (
        energy_ref[:, 0:1],
        first_ref[:, 0:1],
        share_sums(vector * image_ref[...], share),
        share_sums(vector * product_rows, share),
    )
    columns = out_ref.shape[1]
    packed = jnp.zeros((share, columns), F32)
    for q, value in enumerate(sums):
        packed = jnp.where(entries_of(share, columns, share, q), value, packed)
    row = jnp.sum(packed, axis=0, keepdims=True)
    out_ref[...] = jnp.broadcast_to(row, out_ref.shape)


def combine_kernel(sums_ref, first_ref, second_ref, out_ref):
    members, tiles, share, tile = out_ref.shape
    columns = sums_ref.shape[1]
    row = jnp.sum(sums_ref[...], axis=0, keepdims=True)

    def total(q):
        mine = jnp.where(entries_of(share, columns, share, q), row, 0.0)
        return jnp.sum(mine, axis=1, keepdims=True)

    energy, gram_first, gram_mixed, gram_second = (total(q) for q in range(4))
    step_first = energy / gram_first
    mixed_share = gram_mixed / gram_first
    step_second = (gram_mixed - gram_first / energy * gram_first) / (
        gram_second - mixed_share * gram_mixed
    )
    along_first = step_first + step_second * (step_first * mixed_share)
    along_second = step_second * step_first
    for p, t in each_tile(members, tiles):
        here = block(first_ref, p, t, share, tile)[...]
        there = block(second_ref, p, t, share, tile)[...]
        out_ref[p, t] = along_first * here - along_second * there


def finish_kernel(incoming_ref, out_ref):
    members, tiles, share, tile = incoming_ref.shape
    for t in range(tiles):
        rows = incoming_ref[:, t].reshape(members * share, tile)
        out_ref[t * tile : (t + 1) * tile] = jnp.transpose(rows)


def call(kernel, scalars, inputs, outputs, flops=0, in_specs=None, out_specs=None, scratch_shapes=()):
    moved = sum(x.size * x.dtype.itemsize for x in inputs)
    moved += sum(x.size * x.dtype.itemsize for x in outputs)
    single = len(outputs) == 1
    specs = out_specs or [VMEM] * len(outputs)
    return pl.pallas_call(
        kernel,
        out_shape=outputs[0] if single else tuple(outputs),
        in_specs=in_specs or [SMEM] * len(scalars) + [VMEM] * len(inputs),
        out_specs=specs[0] if single else tuple(specs),
        scratch_shapes=scratch_shapes,
        compiler_params=pltpu.CompilerParams(vmem_limit_bytes=20 << 20),
        cost_estimate=pl.CostEstimate(flops=flops, bytes_accessed=moved, transcendentals=0),
    )(*scalars, *inputs)


def body(
    loads,
    coefficient,
    schur_ref,
    schur_inverse,
    coarse_basis,
    partners,
    routes,
    coarse_rows,
    primal_count,
    coarse_inverse,
):
    rows_total, columns = loads.shape[2:]
    peers = partners[0, 0]
    tile_count = peers.shape[1]
    tile = rows_total // tile_count
    members = lax.axis_size("dom")
    groups = lax.axis_size("sub")
    primal_max = coarse_basis.shape[3]
    cap = max(2, (primal_max + groups - 1) // groups)
    stride = cap + 1
    slots = groups * cap
    load_tiles = loads[0, 0]
    inverse_local = schur_inverse[0, 0]

    def shaped(*shape, dtype=F32):
        return jax.ShapeDtypeStruct(shape, dtype)

    share = columns // members
    vector_shape = shaped(columns, rows_total)
    slot_shape = shaped(slots, columns)
    tiles_shape = shaped(members, tile_count, share, tile)
    sum_shape = shaped(share, tile)
    big = 4 * rows_total * rows_total * columns
    thin = 4 * rows_total * slots * columns

    plane = rotated(members, middle_of_plane(members))
    ring = rotated(groups, groups // 2)

    def exchange(tiles):
        return lax.all_to_all(tiles, "dom", 0, 0, tiled=True, axis_index_groups=[plane])

    def shift(values, per_group):
        grouped = values.reshape(groups, 1, per_group * columns)
        moved = lax.all_to_all(grouped, "sub", 0, 0, tiled=True, axis_index_groups=[ring])
        return moved.reshape(groups * per_group, columns)

    given = [
        peers,
        routes.reshape(1, primal_max),
        coarse_rows[0],
        load_tiles,
        coarse_basis[0, 0].T,
    ]
    listed = [pltpu.SMEM(peers.shape, peers.dtype)]
    listed += [pltpu.VMEM(x.shape, x.dtype) for x in given]
    outgoing, slot_basis, wide_basis, labels = call(
        functools.partial(first_kernel, cap),
        [primal_count, coefficient],
        [pltpu.with_memory_space_constraint(x, pltpu.HBM) for x in given],
        [
            shaped(members, tile + 8, columns),
            shaped(slots, rows_total, dtype=BF16),
            shaped(groups * stride, rows_total, dtype=BF16),
            shaped(groups * stride, columns),
        ],
        thin,
        in_specs=[SMEM] * 2 + [pl.BlockSpec(memory_space=pltpu.HBM)] * len(given),
        scratch_shapes=listed
        + [pltpu.VMEM((8, columns), F32), pltpu.SemaphoreType.DMA((len(given) + 1,))],
    )
    residual, outgoing, listed, scale = call(
        first_residual_kernel,
        [peers],
        [load_tiles, exchange(outgoing), wide_basis, labels],
        [
            vector_shape,
            shaped(groups * stride, columns),
            shaped(members, columns, dtype=jnp.int32),
            shaped(columns, columns),
        ],
        2 * thin,
        scratch_shapes=[pltpu.VMEM((rows_total, columns), F32)],
    )
    arrived = shift(outgoing, stride)
    high, low, answer = call(
        functools.partial(first_coarse_kernel, cap, stride),
        [],
        [arrived, coarse_inverse[0, 0]],
        [shaped(slots, slots, dtype=BF16), shaped(slots, slots, dtype=BF16), slot_shape],
        20 * slots * slots * columns,
    )
    returned = shift(answer, cap)
    outgoing, partner = call(
        first_lift_kernel,
        [],
        [inverse_local, slot_basis, returned, residual, listed],
        [
            shaped(members, tile_count + 1, share, tile),
            shaped(members, columns, dtype=jnp.int32),
        ],
        big + thin,
    )
    first, image, outgoing, energy, gram_first = call(
        operate_kernel,
        [partner],
        [exchange(outgoing), schur_ref, scale],
        [
            vector_shape,
            vector_shape,
            tiles_shape,
            sum_shape,
            sum_shape,
        ],
        big,
        scratch_shapes=[pltpu.VMEM(tiles_shape.shape, F32)],
    )
    residual, outgoing = call(
        residual_kernel, [], [exchange(outgoing), slot_basis], [vector_shape, slot_shape], thin
    )
    arrived = shift(outgoing, cap)
    answer = call(coarse_kernel, [], [high, low, arrived], [slot_shape], 6 * slots * slots * columns)
    returned = shift(answer, cap)
    outgoing = call(
        lift_kernel,
        [],
        [inverse_local, slot_basis, returned, residual],
        [tiles_shape],
        big + thin,
    )
    second, sums = call(
        last_kernel,
        [partner],
        [exchange(outgoing), schur_ref, scale, image, energy, gram_first],
        [vector_shape, shaped(groups, columns)],
        big,
    )
    outgoing = call(combine_kernel, [], [shift(sums, 1), first, second], [tiles_shape])
    solution = call(finish_kernel, [], [exchange(outgoing)], [shaped(rows_total, columns)])
    return solution.reshape(1, 1, rows_total, columns)


def solution(mesh):
    return jax.shard_map(
        body,
        mesh=mesh,
        in_specs=(
            P("sub", "dom", None, None),
            P("sub", "dom"),
            P(),
            P("sub", "dom", None, None),
            P("sub", "dom", None, None),
            P("sub", "dom", None, None),
            P("sub", "dom", None, None),
            P("sub", "dom", None),
            P("sub", "dom"),
            P("sub", "dom", None, None),
        ),
        out_specs=P("sub", "dom", None, None),
        check_vma=False,
    )
```
